32 devices in a mesh: lat: 4 (over y, x), lon: 8 (over z, core).
Axes of the slice: x: 2, y: 2, z: 4, core: 2. Of those that a mesh axis runs over, the one named last changes fastest.
Arguments:
- field: bfloat16 [96, 192, 384], P('lat', 'lon'), may hold values from -6 to 6
- cotangent: bfloat16 [96, 192, 384], P('lat', 'lon'), may hold values from -6 to 6
- mix_weight: bfloat16 [3, 384, 384], replicated, may hold values from -0.1875 to 0.1875
- taps: float32 [96, 3, 3, 8], replicated, may hold values from -1.8 to 1.8
- offsets: int32 [96, 3, 8], replicated, may hold values from -8 to 8, as said below
- counts: int32 [96], replicated, may hold values from 1 to 8, as said below
Outputs:
- grad_field: bfloat16 [96, 192, 384], P('lat', 'lon')
- grad_spectra: float32 [2, 384, 384, 384], P(None, 'lat', 'lon')
- grad_mix: float32 [3, 384, 384], replicated
The draws below stay inside these ranges and needn't reach their ends.
Inputs may be any that keep to these rules, and one draw needn't show every extreme that they name: For every row and latitude offset the 8 longitude offsets are distinct. Tap slots of a row at or beyond counts are inactive; the polar rows use all 8.
All inputs are finite; a program needn't handle non-finite values.
Results may differ from the reference program's by a relative error of at most 0.0061.
Values may be sent and summed in bfloat16 or wider, within the bound.
A program may use at most 128 MiB of HBM per device.

```python
import math
import jax
import jax.numpy as jnp
from jax import lax

C = 384
M = 384
L = 384
K = 3
R = 8
S = 8
LB = 32
NLAT = 96
NLON = 192


def reach_rows(row_total):
    row_ids = jnp.arange(row_total, dtype=jnp.int32)
    distance = jnp.minimum(row_ids, row_total - 1 - row_ids)
    return jnp.maximum(1, jnp.minimum(R, 2 * R // (distance + 1)))


def draw_offsets(key, part):
    reach_row = reach_rows(NLAT)
    candidates = jnp.arange(2 * R + 1, dtype=jnp.int32) - R
    scores = jax.random.randint(jax.random.fold_in(key, 11), (NLAT, 3, 2 * R + 1), 0, 1000, dtype=jnp.int32)
    scores = scores * (2 * R + 1) + candidates[None, None, :] + R
    outside = jnp.abs(candidates)[None, None, :] > reach_row[:, None, None]
    scores = jnp.where(outside, scores + 4000 * (2 * R + 1), scores)
    scores = jnp.where(candidates[None, None, :] == reach_row[:, None, None], -2, scores)
    scores = jnp.where(candidates[None, None, :] == -reach_row[:, None, None], -1, scores)
    ranked = jnp.argsort(scores, axis=-1)
    return (ranked[:, :, :S] - R).astype(jnp.int32)


def draw_counts(key, part):
    reach_row = reach_rows(NLAT)
    extra_taps = jax.random.randint(jax.random.fold_in(key, 23), (NLAT,), 0, 3, dtype=jnp.int32)
    return jnp.minimum(jnp.minimum(S, 1 + reach_row + extra_taps), 2 * reach_row + 1).astype(jnp.int32)


def level_of(rng, dims, shards, low, largest):
    def one(position, parts):
        heights = jax.random.uniform(jax.random.fold_in(jax.random.fold_in(rng, 6), position), (parts,), jnp.float32, low / len(shards), largest / len(shards))
        return jnp.repeat(jnp.exp(heights), dims[position] // parts).reshape((-1,) + (1,) * (len(dims) - position - 1))

    loudness = one(*shards[0])
    for cut in shards[1:]:
        loudness = loudness * one(*cut)
    return loudness


def bell_draw(own_key, dims, spread, reach, cuts=(), kind=jnp.bfloat16):
    drawn = spread * jax.random.normal(own_key, dims, jnp.float32)
    if cuts:
        drawn = drawn * level_of(own_key, dims, cuts, -0.22, 0.18)
    return jnp.clip(drawn, -reach, reach).astype(kind)


def setup_inputs(seed: int = 0) -> dict:
    key_of = jax.random.split(jax.random.key(seed), 7)
    field = bell_draw(key_of[0], (NLAT, NLON, C), 1.0, 6.0, ((0, 4), (1, 8)))
    cotangent = bell_draw(key_of[1], (NLAT, NLON, C), 1.0, 6.0, ((0, 4), (1, 8)))
    mix_weight = bell_draw(key_of[2], (K, C, C), (K * C) ** -0.5, 0.1875)
    taps = bell_draw(key_of[3], (NLAT, K, 3, S), 0.3, 1.8, (), jnp.float32)
    offsets = draw_offsets(jax.random.fold_in(key_of[6], 71), 0)
    counts = draw_counts(jax.random.fold_in(key_of[6], 71), 0)
    return dict(field=field, cotangent=cotangent, mix_weight=mix_weight, taps=taps, offsets=offsets, counts=counts)


def live_taps(taps, counts):
    slot_ids = lax.broadcasted_iota(jnp.int32, taps.shape, 3)
    keep_mask = slot_ids < counts[:, None, None, None]
    return jnp.where(keep_mask, taps, jnp.float32(0.0)).astype(jnp.bfloat16)

def dft_table(lon_total, orders):
    columns = lax.broadcasted_iota(jnp.int32, (lon_total,), 0)
    phases = orders[:, None] * columns[None, :] % lon_total
    angles = 2.0 * math.pi / lon_total * phases.astype(jnp.float32)
    return jnp.stack([jnp.cos(angles), -jnp.sin(angles)]).astype(jnp.bfloat16)

def colatitudes(lat_total):
    angles = (lax.broadcasted_iota(jnp.int32, (lat_total,), 0).astype(jnp.float32) + 0.5) * (math.pi / lat_total)
    return (jnp.cos(angles), jnp.log(jnp.sin(angles)))

def seed_logs(order_total):
    degrees = lax.broadcasted_iota(jnp.int32, (order_total,), 0).astype(jnp.float32)
    step_logs = jnp.log((2.0 * degrees + 1.0) / (2.0 * degrees + 2.0))
    prefix = jnp.concatenate([jnp.zeros((1,), jnp.float32), jnp.cumsum(step_logs)[:-1]])
    return 0.5 * jnp.log((2.0 * degrees + 1.0) / (4.0 * math.pi)) + 0.5 * prefix

def advance(degree, previous, earlier, orders, cosines):
    deg_f = jnp.asarray(degree).astype(jnp.float32)
    ord_f = orders.astype(jnp.float32)[:, None]
    higher = (degree > orders)[:, None]
    lower_a = jnp.where(higher, deg_f * deg_f - ord_f * ord_f, 1.0)
    factor_a = jnp.sqrt((4.0 * deg_f * deg_f - 1.0) / lower_a)
    upper_b = jnp.maximum((deg_f - 1.0) * (deg_f - 1.0) - ord_f * ord_f, 0.0)
    lower_b = jnp.maximum(4.0 * (deg_f - 1.0) * (deg_f - 1.0) - 1.0, 1.0)
    factor_b = jnp.sqrt(upper_b / lower_b)
    grown = factor_a * (cosines[None, :] * previous - factor_b * earlier)
    seeded = jnp.where((degree == orders)[:, None], jnp.float32(1.0), jnp.float32(0.0))
    return jnp.where(higher, grown, seeded)

def rescale(previous, earlier, scales):
    biggest = jnp.maximum(jnp.abs(previous), jnp.abs(earlier))
    divisor = jnp.where(biggest > 0.0, biggest, jnp.float32(1.0))
    return (previous / divisor, earlier / divisor, scales + jnp.log(divisor))

def legendre_range(start_block, orders, cosines, logscale, spec_part, result, row_offset, leg_scale):
    state_zero = jnp.zeros(logscale.shape, jnp.float32)

    def block_step(block_idx, loop_state):
        previous, earlier, scales, summed = loop_state
        factor = jnp.exp(scales)
        levels = []
        for inner_step in range(LB):
            degree = block_idx * LB + inner_step
            fresh = advance(degree, previous, earlier, orders, cosines)
            levels.append(fresh * factor)
            earlier, previous = (previous, fresh)
        contrib = jnp.einsum('lmt,pmct->pmcl', jnp.stack(levels), spec_part, precision=lax.Precision.HIGHEST) * leg_scale
        level_start = (block_idx * LB).astype(jnp.int32)
        zero_index = jnp.zeros((), jnp.int32)
        summed = lax.dynamic_update_slice(summed, contrib, (zero_index, jnp.asarray(row_offset).astype(jnp.int32), zero_index, level_start))
        previous, earlier, scales = rescale(previous, earlier, scales)
        return (previous, earlier, scales, summed)
    return lax.fori_loop(start_block, L // LB, block_step, (state_zero, state_zero, logscale, result))[3]

def reference(field, cotangent, mix_weight, taps, offsets, counts):
    live_table = live_taps(taps, counts)
    field_pad = jnp.pad(field, ((1, 1), (0, 0), (0, 0)))
    columns = jnp.arange(NLON, dtype=jnp.int32)
    row_ids = jnp.arange(NLAT, dtype=jnp.int32)

    def forward_row(mix_total, row_id):
        rows_three = lax.dynamic_slice_in_dim(field_pad, row_id, 3, 0)
        row_taps = live_table[row_id]
        row_shifts = offsets[row_id]
        summed = jnp.zeros((NLON, K, C), jnp.float32)
        for lat_step in range(3):
            for tap_slot in range(S):
                index_map = (columns + row_shifts[lat_step, tap_slot]) % NLON
                moved_rows = jnp.take(rows_three[lat_step], index_map, axis=0).astype(jnp.float32)
                summed = summed + moved_rows[:, None, :] * row_taps[:, lat_step, tap_slot].astype(jnp.float32)[None, :, None]
        response = lax.optimization_barrier(summed.astype(jnp.bfloat16)).astype(jnp.float32)
        grad_row = cotangent[row_id].astype(jnp.float32)
        mix_total = mix_total + jnp.einsum('fkc,fd->kcd', response, grad_row)
        return (mix_total, None)
    mix_total, ignored = lax.scan(forward_row, jnp.zeros((K, C, C), jnp.float32), row_ids)
    grad_mix = mix_total * (1.0 / math.sqrt(NLAT * NLON))
    weight_mat = jnp.transpose(mix_weight, (2, 0, 1)).reshape(C, K * C)

    def basis_row(row_vals):
        return jnp.dot(row_vals, weight_mat, preferred_element_type=jnp.float32).reshape(NLON, K, C).astype(jnp.bfloat16)
    grad_basis = lax.map(basis_row, cotangent)
    live_pad = jnp.pad(live_table, ((1, 1), (0, 0), (0, 0), (0, 0)))
    shift_pad = jnp.pad(offsets, ((1, 1), (0, 0), (0, 0)))

    def backward_row(row_id):
        summed = cotangent[row_id].astype(jnp.float32)
        for lat_step in range(3):
            source = row_id - lat_step + 1
            basis_one = grad_basis[jnp.clip(source, 0, NLAT - 1)]
            row_taps = live_pad[source + 1]
            row_shifts = shift_pad[source + 1]
            for tap_slot in range(S):
                index_map = (columns - row_shifts[lat_step, tap_slot]) % NLON
                moved_rows = jnp.take(basis_one, index_map, axis=0).astype(jnp.float32)
                summed = summed + jnp.einsum('fkc,k->fc', moved_rows, row_taps[:, lat_step, tap_slot].astype(jnp.float32))
        return summed.astype(jnp.bfloat16)
    grad_field = lax.map(backward_row, row_ids)
    dft_rows = dft_table(NLON, jnp.arange(M, dtype=jnp.int32))
    spectra = (jnp.einsum('tfc,pmf->pmct', grad_field.astype(jnp.float32), dft_rows.astype(jnp.float32)) * (1.0 / math.sqrt(NLON))).astype(jnp.bfloat16)
    cosines, log_sines = colatitudes(NLAT)
    orders = jnp.arange(M, dtype=jnp.int32)
    logscale = seed_logs(M)[:, None] + orders.astype(jnp.float32)[:, None] * log_sines[None, :]
    grad_spectra = legendre_range(0, orders, cosines, logscale, spectra.astype(jnp.float32), jnp.zeros((2, M, C, L), jnp.float32), 0, math.sqrt(4.0 * math.pi / NLAT))
    return (grad_field, grad_spectra, grad_mix)
```

```python
import functools
import math

import jax
import jax.numpy as jnp
from jax import lax
from jax.experimental import pallas as pl
from jax.experimental.pallas import tpu as pltpu
from jax.sharding import PartitionSpec as P

M = 384
L = 384
K = 3
R = 8
S = 8
LB = 32
MSTEP = 8
VMEM_BYTES = 56 * 1024 * 1024


def round_up(value, unit):
    return -(-value // unit) * unit


def live_taps(taps, counts):
    slot_ids = lax.broadcasted_iota(jnp.int32, taps.shape, 3)
    keep_mask = slot_ids < counts[:, None, None, None]
    return jnp.where(keep_mask, taps, jnp.float32(0.0)).astype(jnp.bfloat16)


def dft_table(lon_total, orders):
    columns = lax.broadcasted_iota(jnp.int32, (lon_total,), 0)
    phases = orders[:, None] * columns[None, :] % lon_total
    angles = 2.0 * math.pi / lon_total * phases.astype(jnp.float32)
    return jnp.stack([jnp.cos(angles), -jnp.sin(angles)]).astype(jnp.bfloat16)


def colatitudes(lat_total):
    angles = (lax.broadcasted_iota(jnp.int32, (lat_total,), 0).astype(jnp.float32) + 0.5) * (
        math.pi / lat_total
    )
    return (jnp.cos(angles), jnp.log(jnp.sin(angles)))


def seed_logs(order_total):
    degrees = lax.broadcasted_iota(jnp.int32, (order_total,), 0).astype(jnp.float32)
    step_logs = jnp.log((2.0 * degrees + 1.0) / (2.0 * degrees + 2.0))
    prefix = jnp.concatenate([jnp.zeros((1,), jnp.float32), jnp.cumsum(step_logs)[:-1]])
    return 0.5 * jnp.log((2.0 * degrees + 1.0) / (4.0 * math.pi)) + 0.5 * prefix


def legendre_kernel(first_ref, cos_ref, seed_ref, table_ref, prev_ref, early_ref, scale_ref, *stage_refs):
    step = pl.program_id(0)
    rows, width = seed_ref.shape
    first = first_ref[0]

    @pl.when(step == 0)
    def _():
        prev_ref[...] = jnp.zeros_like(prev_ref)
        early_ref[...] = jnp.zeros_like(early_ref)
        scale_ref[...] = seed_ref[...]

    chunk = 48 if rows % 48 == 0 else 8
    cosines = cos_ref[...]
    for begin in range(0, rows, chunk):
        span = slice(begin, begin + chunk)
        order_i = lax.broadcasted_iota(jnp.int32, (chunk, LB), 0) + (first + begin)
        degree_i = lax.broadcasted_iota(jnp.int32, (chunk, LB), 1) + step * LB
        order = order_i.astype(jnp.float32)
        degree = degree_i.astype(jnp.float32)
        higher = degree_i > order_i
        lower_a = jnp.where(higher, degree * degree - order * order, 1.0)
        factor_a = jnp.sqrt((4.0 * degree * degree - 1.0) / lower_a)
        upper_b = jnp.maximum((degree - 1.0) * (degree - 1.0) - order * order, 0.0)
        lower_b = jnp.maximum(4.0 * (degree - 1.0) * (degree - 1.0) - 1.0, 1.0)
        factor_b = jnp.sqrt(upper_b / lower_b)
        gain = jnp.where(higher, factor_a, 0.0)
        back = jnp.where(higher, factor_a * factor_b, 0.0)
        wide_order = lax.broadcasted_iota(jnp.int32, (chunk, width), 0) + (first + begin)
        previous = prev_ref[span, :]
        earlier = early_ref[span, :]
        scales = scale_ref[span, :]
        factor = jnp.exp(scales)
        for inner in range(LB):
            seeded = jnp.where(wide_order == step * LB + inner, 1.0, 0.0)
            fresh = (
                gain[:, inner : inner + 1] * (cosines * previous)
                - back[:, inner : inner + 1] * earlier
                + seeded
            )
            level = fresh * factor
            for tile, stage_ref in enumerate(stage_refs):
                stage_ref[pl.ds(begin * LB + inner, chunk, stride=LB), :] = level[:, tile * 128 : tile * 128 + 128]
            earlier, previous = previous, fresh
        biggest = jnp.maximum(jnp.abs(previous), jnp.abs(earlier))
        divisor = jnp.where(biggest > 0.0, biggest, 1.0)
        prev_ref[span, :] = previous / divisor
        early_ref[span, :] = earlier / divisor
        scale_ref[span, :] = scales + jnp.log(divisor)
    for tile, stage_ref in enumerate(stage_refs):
        staged = stage_ref[...].reshape(rows, LB, 128).astype(jnp.bfloat16)
        table_ref[:, :, tile * 128 : tile * 128 + 128] = staged


def legendre_table(first_order, cosines, logscale):
    rows, lat_total = logscale.shape
    width = round_up(lat_total, 128)
    spare = width - lat_total
    cos_pad = jnp.pad(cosines, (0, spare))[None, :]
    seed_pad = jnp.pad(logscale, ((0, 0), (0, spare)), constant_values=-1.0e4)
    stage_rows = rows * LB
    return pl.pallas_call(
        legendre_kernel,
        grid=(L // LB,),
        in_specs=[
            pl.BlockSpec(memory_space=pltpu.SMEM),
            pl.BlockSpec((1, width), lambda i: (0, 0)),
            pl.BlockSpec((rows, width), lambda i: (0, 0)),
        ],
        out_specs=pl.BlockSpec((rows, LB, width), lambda i: (0, i, 0)),
        out_shape=jax.ShapeDtypeStruct((rows, L, width), jnp.bfloat16),
        scratch_shapes=[pltpu.VMEM((rows, width), jnp.float32)] * 3
        + [pltpu.VMEM((stage_rows, 128), jnp.float32)] * (width // 128),
        compiler_params=pltpu.CompilerParams(vmem_limit_bytes=VMEM_BYTES),
        cost_estimate=pl.CostEstimate(
            flops=rows * L * width * 10, bytes_accessed=rows * L * width * 2, transcendentals=0
        ),
        name="legendre_table",
    )(first_order.reshape(1), cos_pad, seed_pad)


def synthesis_kernel(lon_total, lat_total, dft_ref, grid_ref, table_ref, out_ref, modes_ref):
    step = pl.program_id(0)
    bands, _, packed = grid_ref.shape
    rows = dft_ref.shape[0] // 2
    chans = out_ref.shape[2]
    lat_dev = packed // chans
    width = table_ref.shape[2]

    @pl.when(step == 0)
    def _():
        @pl.loop(0, bands)
        def _(band):
            modes = jnp.dot(dft_ref[...], grid_ref[band], preferred_element_type=jnp.float32)
            modes = (modes * (1.0 / math.sqrt(lon_total))).astype(jnp.bfloat16).astype(jnp.float32)
            for lat in range(lat_dev):
                dest = pl.ds(pl.multiple_of((band * lat_dev + lat) * rows, 8), rows)
                lanes = slice(lat * chans, (lat + 1) * chans)
                modes_ref[dest, 0:chans] = modes[0:rows, lanes]
                modes_ref[dest, chans : 2 * chans] = modes[rows : 2 * rows, lanes]

    leg_scale = math.sqrt(4.0 * math.pi / lat_total)
    for inner in range(MSTEP):
        picked = modes_ref[pl.ds(step * MSTEP + inner, lat_total, stride=rows), :]
        if width > lat_total:
            spare = jnp.zeros((width - lat_total, picked.shape[1]), jnp.float32)
            picked = jnp.concatenate([picked, spare], axis=0)
        turned = picked.T[0 : 2 * chans].astype(jnp.bfloat16)
        product = lax.dot_general(
            turned, table_ref[inner], (((1,), (1,)), ((), ())), preferred_element_type=jnp.float32
        )
        product = product * leg_scale
        out_ref[0, inner] = product[0:chans]
        out_ref[1, inner] = product[chans : 2 * chans]


def synthesis(dft_rows, gathered, table, chans, lat_total, lon_total):
    rows = table.shape[0]
    width = table.shape[2]
    whole = lambda i: (0, 0)
    return pl.pallas_call(
        functools.partial(synthesis_kernel, lon_total, lat_total),
        grid=(rows // MSTEP,),
        in_specs=[
            pl.BlockSpec(dft_rows.shape, whole),
            pl.BlockSpec(gathered.shape, lambda i: (0, 0, 0), pipeline_mode=pl.Buffered(1)),
            pl.BlockSpec((MSTEP, L, width), lambda i: (i, 0, 0)),
        ],
        out_specs=pl.BlockSpec((2, MSTEP, chans, L), lambda i: (0, i, 0, 0)),
        out_shape=jax.ShapeDtypeStruct((2, rows, chans, L), jnp.float32),
        scratch_shapes=[pltpu.VMEM((lat_total * rows, 128), jnp.float32)],
        compiler_params=pltpu.CompilerParams(vmem_limit_bytes=VMEM_BYTES),
        name="dft_synthesis",
    )(dft_rows, gathered, table)


def grid_kernel(
    lon_count, ext_ref, cot_ref, weight_ref, tap_own_ref, shift_own_ref, tap_back_ref, shift_back_ref,
    response_ref, field_ref, send_ref, moved_ref, total_ref, packed_ref,
):
    lat_dev = tap_own_ref.shape[0]
    cells, channels = cot_ref.shape
    lon_dev = cells // lat_dev
    lanes = tap_own_ref.shape[2]
    ext_width = lanes // 3
    lane = lax.broadcasted_iota(jnp.int32, (lon_dev, lanes), 1)
    lane = jnp.where(lane >= 2 * ext_width, lane - 2 * ext_width, jnp.where(lane >= ext_width, lane - ext_width, lane))
    relative = lane - lax.broadcasted_iota(jnp.int32, (lon_dev, lanes), 0) - R

    def bands(row, tap_ref, shift_ref):
        summed = [jnp.zeros((lon_dev, lanes), jnp.float32)] * K
        for slot in range(S):
            hit = relative == shift_ref[row, slot : slot + 1, :]
            for k in range(K):
                tap = tap_ref[row, k * S + slot : k * S + slot + 1, :]
                summed[k] = summed[k] + jnp.where(hit, tap, 0.0)
        return jnp.concatenate(summed, axis=0).astype(jnp.bfloat16)

    @pl.loop(0, lat_dev // 2)
    def _(pair):
        own, back = [], []
        for half in range(2):
            row = pair * 2 + half
            rows = pl.ds(pl.multiple_of(row * ext_width, 16), lanes)
            own.append(
                jnp.dot(
                    bands(row, tap_own_ref, shift_own_ref), ext_ref[rows, 0:channels],
                    preferred_element_type=jnp.float32,
                )
            )
            back.append(
                jnp.dot(
                    bands(row, tap_back_ref, shift_back_ref), ext_ref[rows, channels : 2 * channels],
                    preferred_element_type=jnp.float32,
                )
            )
        dest = pl.ds(pl.multiple_of(pair * 2 * lon_dev, 16), 2 * lon_dev)
        for k in range(K):
            part = slice(k * lon_dev, (k + 1) * lon_dev)
            cols = slice(k * channels, (k + 1) * channels)
            response_ref[dest, cols] = jnp.concatenate([own[0][part], own[1][part]], axis=0).astype(jnp.bfloat16)
            moved_ref[dest, cols] = jnp.concatenate([back[0][part], back[1][part]], axis=0).astype(jnp.bfloat16)

    total = cot_ref[...].astype(jnp.float32)
    for k in range(K):
        total = total + lax.dot_general(
            moved_ref[:, k * channels : (k + 1) * channels], weight_ref[k],
            (((1,), (1,)), ((), ())), preferred_element_type=jnp.float32,
        )
    rounded = total.astype(jnp.bfloat16)
    field_ref[...] = rounded
    total_ref[...] = rounded.astype(jnp.float32)
    chans = channels // lon_count
    for lat in range(lat_dev):
        for dest in range(lon_count):
            packed_ref[dest, :, lat * chans : (lat + 1) * chans] = total_ref[
                lat * lon_dev : (lat + 1) * lon_dev, dest * chans : (dest + 1) * chans
            ]
    send_ref[...] = packed_ref[...].astype(jnp.bfloat16)


def grid_part(ext, cot, mix_weight, tap_own, shift_own, tap_back, shift_back, lon_count):
    cells, channels = cot.shape
    lat_dev = tap_own.shape[0]
    lon_dev = cells // lat_dev
    packed = (lon_count, lon_dev, lat_dev * (channels // lon_count))
    return pl.pallas_call(
        functools.partial(grid_kernel, lon_count),
        in_specs=[pl.BlockSpec(memory_space=pltpu.VMEM)] * 7,
        out_specs=[pl.BlockSpec(memory_space=pltpu.VMEM)] * 3,
        out_shape=[
            jax.ShapeDtypeStruct((cells, K * channels), jnp.bfloat16),
            jax.ShapeDtypeStruct((cells, channels), jnp.bfloat16),
            jax.ShapeDtypeStruct(packed, jnp.bfloat16),
        ],
        scratch_shapes=[
            pltpu.VMEM((cells, K * channels), jnp.bfloat16),
            pltpu.VMEM((cells, channels), jnp.float32),
            pltpu.VMEM(packed, jnp.float32),
        ],
        compiler_params=pltpu.CompilerParams(vmem_limit_bytes=VMEM_BYTES),
        name="grid_part",
    )(ext, cot, mix_weight, tap_own, shift_own, tap_back, shift_back)


def swap_edges(shard, axis, dim, width, wrap):
    devices, length = lax.axis_size(axis), shard.shape[dim]
    up = [(i, (i + 1) % devices) for i in range(devices if wrap else devices - 1)]
    down = [(j, i) for i, j in up]
    before = lax.ppermute(lax.slice_in_dim(shard, length - width, length, axis=dim), axis, up)
    after = lax.ppermute(lax.slice_in_dim(shard, 0, width, axis=dim), axis, down)
    return before, after


def spread(values, ext_width):
    return jnp.repeat(values, ext_width, axis=-1)


def on_device(field, cotangent, mix_weight, taps, offsets, counts):
    lat_dev, lon_dev, channels = field.shape
    lat_count = lax.axis_size("lat")
    lon_count = lax.axis_size("lon")
    total_lat = lat_dev * lat_count
    total_lon = lon_dev * lon_count
    lat_pos = lax.axis_index("lat")
    block_rows = M // lat_count
    chans = channels // lon_count
    first_row = lat_pos * lat_dev
    ext_width = round_up(lon_dev + 2 * R, 16)

    both = jnp.concatenate([field, cotangent], axis=2)
    before, after = swap_edges(both, "lon", 1, R, True)
    spare = jnp.zeros((lat_dev, ext_width - lon_dev - 2 * R, 2 * channels), jnp.bfloat16)
    wide = jnp.concatenate([before, both, after, spare], axis=1)
    above, below = swap_edges(wide, "lat", 0, 1, False)
    ext = jnp.concatenate([above, wide, below], axis=0).reshape((lat_dev + 2) * ext_width, 2 * channels)

    live = live_taps(taps, counts).astype(jnp.float32)
    live_ext = lax.dynamic_slice_in_dim(jnp.pad(live, ((1, 1), (0, 0), (0, 0), (0, 0))), first_row, lat_dev + 2, 0)
    shift_ext = lax.dynamic_slice_in_dim(jnp.pad(offsets, ((1, 1), (0, 0), (0, 0))), first_row, lat_dev + 2, 0)
    tap_own = spread(jnp.transpose(live_ext[1:-1], (0, 1, 3, 2)), ext_width).reshape(lat_dev, K * S, 3 * ext_width)
    shift_own = spread(jnp.transpose(shift_ext[1:-1], (0, 2, 1)), ext_width)
    live_back = jnp.stack([live_ext[a : a + lat_dev, :, 2 - a, :] for a in range(3)], axis=-1)
    shift_back = jnp.stack([-shift_ext[a : a + lat_dev, 2 - a, :] for a in range(3)], axis=-1)
    tap_back = spread(live_back, ext_width).reshape(lat_dev, K * S, 3 * ext_width)
    shift_back = spread(shift_back, ext_width)

    cot_flat = cotangent.reshape(lat_dev * lon_dev, channels)
    response, grad_field, packed = grid_part(
        ext, cot_flat, mix_weight, tap_own, shift_own, tap_back, shift_back, lon_count
    )

    cosines, log_sines = colatitudes(total_lat)
    orders = lat_pos * block_rows + lax.broadcasted_iota(jnp.int32, (block_rows,), 0)
    own_logs = lax.dynamic_slice_in_dim(seed_logs(M), lat_pos * block_rows, block_rows, 0)
    logscale = own_logs[:, None] + orders.astype(jnp.float32)[:, None] * log_sines[None, :]
    table = legendre_table((lat_pos * block_rows).astype(jnp.int32), cosines, logscale)
    dft_rows = dft_table(total_lon, orders).reshape(2 * block_rows, total_lon)

    columns = lax.all_to_all(packed, "lon", split_axis=0, concat_axis=0, tiled=True)
    columns = columns.reshape(total_lon, lat_dev * chans)
    gathered = lax.all_gather(columns, "lat", axis=0, tiled=False)
    grad_spectra = synthesis(dft_rows, gathered, table, chans, total_lat, total_lon)

    mix_local = lax.dot_general(
        response, cot_flat, (((0,), (0,)), ((), ())), preferred_element_type=jnp.float32
    ) * (1.0 / math.sqrt(total_lat * total_lon))
    grad_mix = lax.psum(mix_local, ("lat", "lon")).reshape(K, channels, channels)
    return (grad_field.reshape(lat_dev, lon_dev, channels), grad_spectra, grad_mix)


def solution(mesh):
    placed = (P("lat", "lon", None), P("lat", "lon", None), P(), P(), P(), P())
    return jax.shard_map(
        on_device,
        mesh=mesh,
        in_specs=placed,
        out_specs=(P("lat", "lon", None), P(None, "lat", "lon", None), P()),
        check_vma=False,
    )
```

```python
import functools
import math

import jax
import jax.numpy as jnp
from jax import lax
from jax.experimental import pallas as pl
from jax.experimental.pallas import tpu as pltpu
from jax.sharding import PartitionSpec as P

M = 384
L = 384
K = 3
R = 8
S = 8
LB = 32
MSTEP = 8
DEGREES = 128
PITCH = LB + 1
VMEM_BYTES = 56 * 1024 * 1024


def round_up(value, unit):
    return -(-value // unit) * unit


def live_taps(taps, counts):
    slot_ids = lax.broadcasted_iota(jnp.int32, taps.shape, 3)
    keep_mask = slot_ids < counts[:, None, None, None]
    return jnp.where(keep_mask, taps, jnp.float32(0.0)).astype(jnp.bfloat16)


def dft_table(lon_total, orders):
    columns = lax.broadcasted_iota(jnp.int32, (lon_total,), 0)
    phases = orders[:, None] * columns[None, :] % lon_total
    angles = 2.0 * math.pi / lon_total * phases.astype(jnp.float32)
    return jnp.stack([jnp.cos(angles), -jnp.sin(angles)]).astype(jnp.bfloat16)


def colatitudes(lat_total):
    angles = (lax.broadcasted_iota(jnp.int32, (lat_total,), 0).astype(jnp.float32) + 0.5) * (
        math.pi / lat_total
    )
    return (jnp.cos(angles), jnp.log(jnp.sin(angles)))


def seed_logs(order_total):
    degrees = lax.broadcasted_iota(jnp.int32, (order_total,), 0).astype(jnp.float32)
    step_logs = jnp.log((2.0 * degrees + 1.0) / (2.0 * degrees + 2.0))
    prefix = jnp.concatenate([jnp.zeros((1,), jnp.float32), jnp.cumsum(step_logs)[:-1]])
    return 0.5 * jnp.log((2.0 * degrees + 1.0) / (4.0 * math.pi)) + 0.5 * prefix


def legendre_kernel(start_block, first_ref, cos_ref, prev_in, early_in, scale_in, table_ref, prev_ref, early_ref, scale_ref, *stage_refs):
    step = start_block + pl.program_id(0)
    rows, width = scale_in.shape
    first = first_ref[0]

    @pl.when(pl.program_id(0) == 0)
    def _():
        prev_ref[...] = prev_in[...]
        early_ref[...] = early_in[...]
        scale_ref[...] = scale_in[...]

    chunk = 48 if rows % 48 == 0 else 8
    cosines = cos_ref[...]
    for begin in range(0, rows, chunk):
        span = slice(begin, begin + chunk)
        order_i = lax.broadcasted_iota(jnp.int32, (chunk, LB), 0) + (first + begin)
        degree_i = lax.broadcasted_iota(jnp.int32, (chunk, LB), 1) + step * LB
        order = order_i.astype(jnp.float32)
        degree = degree_i.astype(jnp.float32)
        higher = degree_i > order_i
        lower_a = jnp.where(higher, degree * degree - order * order, 1.0)
        factor_a = jnp.sqrt((4.0 * degree * degree - 1.0) / lower_a)
        upper_b = jnp.maximum((degree - 1.0) * (degree - 1.0) - order * order, 0.0)
        lower_b = jnp.maximum(4.0 * (degree - 1.0) * (degree - 1.0) - 1.0, 1.0)
        factor_b = jnp.sqrt(upper_b / lower_b)
        gain = jnp.where(higher, factor_a, 0.0)
        back = jnp.where(higher, factor_a * factor_b, 0.0)
        wide_order = lax.broadcasted_iota(jnp.int32, (chunk, width), 0) + (first + begin)
        previous = prev_ref[span, :]
        earlier = early_ref[span, :]
        scales = scale_ref[span, :]
        factor = jnp.exp(scales)
        for inner in range(LB):
            seeded = jnp.where(wide_order == step * LB + inner, 1.0, 0.0)
            fresh = (
                gain[:, inner : inner + 1] * (cosines * previous)
                - back[:, inner : inner + 1] * earlier
                + seeded
            )
            level = fresh * factor
            for tile, stage_ref in enumerate(stage_refs):
                stage_ref[pl.ds(begin * PITCH + inner, chunk, stride=PITCH), :] = level[:, tile * 128 : tile * 128 + 128]
            earlier, previous = previous, fresh
        biggest = jnp.maximum(jnp.abs(previous), jnp.abs(earlier))
        divisor = jnp.where(biggest > 0.0, biggest, 1.0)
        prev_ref[span, :] = previous / divisor
        early_ref[span, :] = earlier / divisor
        scale_ref[span, :] = scales + jnp.log(divisor)
    for tile, stage_ref in enumerate(stage_refs):
        for row in range(rows):
            staged = stage_ref[row * PITCH : row * PITCH + LB, :]
            table_ref[row, :, tile * 128 : tile * 128 + 128] = staged.astype(jnp.bfloat16)


def legendre_state(cosines, logscale):
    rows, lat_total = logscale.shape
    spare = round_up(lat_total, 128) - lat_total
    cos_pad = jnp.pad(cosines, (0, spare))[None, :]
    seed_pad = jnp.pad(logscale, ((0, 0), (0, spare)), constant_values=-1.0e4)
    nothing = jnp.zeros_like(seed_pad)
    return cos_pad, (nothing, nothing, seed_pad)


def legendre_table(first_order, cos_pad, state, start_block):
    rows, width = state[0].shape
    plain = pl.BlockSpec((rows, width), lambda i: (0, 0))
    held = jax.ShapeDtypeStruct((rows, width), jnp.float32)
    outs = pl.pallas_call(
        functools.partial(legendre_kernel, start_block),
        grid=(DEGREES // LB,),
        in_specs=[
            pl.BlockSpec(memory_space=pltpu.SMEM),
            pl.BlockSpec((1, width), lambda i: (0, 0)),
            plain,
            plain,
            plain,
        ],
        out_specs=[pl.BlockSpec((rows, LB, width), lambda i: (0, i, 0)), plain, plain, plain],
        out_shape=[jax.ShapeDtypeStruct((rows, DEGREES, width), jnp.bfloat16), held, held, held],
        scratch_shapes=[pltpu.VMEM((rows * PITCH, 128), jnp.float32)] * (width // 128),
        compiler_params=pltpu.CompilerParams(vmem_limit_bytes=VMEM_BYTES),
        cost_estimate=pl.CostEstimate(
            flops=rows * DEGREES * width * 5000, bytes_accessed=rows * DEGREES * width * 2, transcendentals=0
        ),
        name="legendre_table",
    )(first_order.reshape(1), cos_pad, *state)
    return outs[0], tuple(outs[1:])


def synthesis_kernel(lon_total, lat_total, band_count, *refs):
    step = pl.program_id(0)
    band_ref, dft_ref = refs[:2]
    grid_refs = refs[2 : 2 + band_count]
    table_refs = refs[2 + band_count : -2]
    out_ref, modes_ref = refs[-2:]
    packed = grid_refs[0].shape[1]
    rows = dft_ref.shape[0] // 2
    chans = out_ref.shape[2]
    lat_dev = packed // chans
    width = table_refs[0].shape[2]

    @pl.when(step == 0)
    def _():
        for source, grid_ref in enumerate(grid_refs):
            band = band_ref[source]
            modes = jnp.dot(dft_ref[...], grid_ref[...], preferred_element_type=jnp.float32)
            modes = (modes * (1.0 / math.sqrt(lon_total))).astype(jnp.bfloat16).astype(jnp.float32)
            for lat in range(lat_dev):
                dest = pl.ds(pl.multiple_of((band * lat_dev + lat) * rows, 8), rows)
                lanes = slice(lat * chans, (lat + 1) * chans)
                modes_ref[dest, 0:chans] = modes[0:rows, lanes]
                modes_ref[dest, chans : 2 * chans] = modes[rows : 2 * rows, lanes]

    leg_scale = math.sqrt(4.0 * math.pi / lat_total)
    for inner in range(MSTEP):
        picked = modes_ref[pl.ds(step * MSTEP + inner, lat_total, stride=rows), :]
        if width > lat_total:
            spare = jnp.zeros((width - lat_total, picked.shape[1]), jnp.float32)
            picked = jnp.concatenate([picked, spare], axis=0)
        turned = picked.T[0 : 2 * chans].astype(jnp.bfloat16)
        product = lax.dot_general(
            turned,
            jnp.concatenate([table_ref[inner] for table_ref in table_refs], axis=0),
            (((1,), (1,)), ((), ())),
            preferred_element_type=jnp.float32,
        )
        product = product * leg_scale
        out_ref[0, inner] = product[0:chans]
        out_ref[1, inner] = product[chans : 2 * chans]


def synthesis(bands, dft_rows, columns, tables, chans, lat_total, lon_total):
    rows, _, width = tables[0].shape
    whole = lambda i: (0, 0)
    table_spec = pl.BlockSpec((MSTEP, DEGREES, width), lambda i: (i, 0, 0))
    grid_spec = pl.BlockSpec(columns[0].shape, whole, pipeline_mode=pl.Buffered(1))
    return pl.pallas_call(
        functools.partial(synthesis_kernel, lon_total, lat_total, len(columns)),
        grid=(rows // MSTEP,),
        in_specs=[pl.BlockSpec(memory_space=pltpu.SMEM), pl.BlockSpec(dft_rows.shape, whole)]
        + [grid_spec] * len(columns)
        + [table_spec] * len(tables),
        out_specs=pl.BlockSpec((2, MSTEP, chans, L), lambda i: (0, i, 0, 0)),
        out_shape=jax.ShapeDtypeStruct((2, rows, chans, L), jnp.float32),
        scratch_shapes=[pltpu.VMEM((lat_total * rows, 128), jnp.float32)],
        compiler_params=pltpu.CompilerParams(vmem_limit_bytes=VMEM_BYTES),
        cost_estimate=pl.CostEstimate(
            flops=20_000_000_000, bytes_accessed=8 * rows * chans * L, transcendentals=0
        ),
        name="dft_synthesis",
    )(bands, dft_rows, *columns, *tables)


def grid_kernel(
    lon_count, ext_ref, cot_ref, weight_ref, tap_own_ref, shift_own_ref, tap_back_ref, shift_back_ref,
    response_ref, field_ref, send_ref, moved_ref, total_ref, packed_ref,
):
    lat_dev = tap_own_ref.shape[0]
    cells, channels = cot_ref.shape
    lon_dev = cells // lat_dev
    lanes = tap_own_ref.shape[2]
    ext_width = lanes // 3
    lane = lax.broadcasted_iota(jnp.int32, (lon_dev, lanes), 1)
    lane = jnp.where(lane >= 2 * ext_width, lane - 2 * ext_width, jnp.where(lane >= ext_width, lane - ext_width, lane))
    relative = lane - lax.broadcasted_iota(jnp.int32, (lon_dev, lanes), 0) - R

    def bands(row, tap_ref, shift_ref):
        summed = [jnp.zeros((lon_dev, lanes), jnp.float32)] * K
        for slot in range(S):
            hit = relative == shift_ref[row, slot : slot + 1, :]
            for k in range(K):
                tap = tap_ref[row, k * S + slot : k * S + slot + 1, :]
                summed[k] = summed[k] + jnp.where(hit, tap, 0.0)
        return jnp.concatenate(summed, axis=0).astype(jnp.bfloat16)

    @pl.loop(0, lat_dev // 2)
    def _(pair):
        own, back = [], []
        for half in range(2):
            row = pair * 2 + half
            rows = pl.ds(pl.multiple_of(row * ext_width, 16), lanes)
            own.append(
                jnp.dot(
                    bands(row, tap_own_ref, shift_own_ref), ext_ref[rows, 0:channels],
                    preferred_element_type=jnp.float32,
                )
            )
            back.append(
                jnp.dot(
                    bands(row, tap_back_ref, shift_back_ref), ext_ref[rows, channels : 2 * channels],
                    preferred_element_type=jnp.float32,
                )
            )
        dest = pl.ds(pl.multiple_of(pair * 2 * lon_dev, 16), 2 * lon_dev)
        for k in range(K):
            part = slice(k * lon_dev, (k + 1) * lon_dev)
            cols = slice(k * channels, (k + 1) * channels)
            response_ref[dest, cols] = jnp.concatenate([own[0][part], own[1][part]], axis=0).astype(jnp.bfloat16)
            moved_ref[dest, cols] = jnp.concatenate([back[0][part], back[1][part]], axis=0).astype(jnp.bfloat16)

    total = cot_ref[...].astype(jnp.float32)
    for k in range(K):
        total = total + lax.dot_general(
            moved_ref[:, k * channels : (k + 1) * channels], weight_ref[k],
            (((1,), (1,)), ((), ())), preferred_element_type=jnp.float32,
        )
    rounded = total.astype(jnp.bfloat16)
    field_ref[...] = rounded
    total_ref[...] = rounded.astype(jnp.float32)
    chans = channels // lon_count
    for lat in range(lat_dev):
        for dest in range(lon_count):
            packed_ref[dest, :, lat * chans : (lat + 1) * chans] = total_ref[
                lat * lon_dev : (lat + 1) * lon_dev, dest * chans : (dest + 1) * chans
            ]
    send_ref[...] = packed_ref[...].astype(jnp.bfloat16)


def grid_part(ext, cot, mix_weight, tap_own, shift_own, tap_back, shift_back, lon_count):
    cells, channels = cot.shape
    lat_dev = tap_own.shape[0]
    lon_dev = cells // lat_dev
    packed = (lon_count, lon_dev, lat_dev * (channels // lon_count))
    return pl.pallas_call(
        functools.partial(grid_kernel, lon_count),
        in_specs=[pl.BlockSpec(memory_space=pltpu.VMEM)] * 7,
        out_specs=[pl.BlockSpec(memory_space=pltpu.VMEM)] * 3,
        out_shape=[
            jax.ShapeDtypeStruct((cells, K * channels), jnp.bfloat16),
            jax.ShapeDtypeStruct((cells, channels), jnp.bfloat16),
            jax.ShapeDtypeStruct(packed, jnp.bfloat16),
        ],
        scratch_shapes=[
            pltpu.VMEM((cells, K * channels), jnp.bfloat16),
            pltpu.VMEM((cells, channels), jnp.float32),
            pltpu.VMEM(packed, jnp.float32),
        ],
        compiler_params=pltpu.CompilerParams(vmem_limit_bytes=VMEM_BYTES),
        name="grid_part",
    )(ext, cot, mix_weight, tap_own, shift_own, tap_back, shift_back)


def swap_edges(shard, axis, dim, width, wrap):
    devices, length = lax.axis_size(axis), shard.shape[dim]
    up = [(i, (i + 1) % devices) for i in range(devices if wrap else devices - 1)]
    down = [(j, i) for i, j in up]
    before = lax.ppermute(lax.slice_in_dim(shard, length - width, length, axis=dim), axis, up)
    after = lax.ppermute(lax.slice_in_dim(shard, 0, width, axis=dim), axis, down)
    return before, after


def partner(position, turn, count):
    if count & (count - 1) == 0:
        return position ^ turn
    return (position + turn) % count


def source_of(position, turn, count):
    if count & (count - 1) == 0:
        return position ^ turn
    return (position + count - turn) % count


def swap_with(value, turn, count):
    return lax.ppermute(value, "lat", [(i, partner(i, turn, count)) for i in range(count)])


def spread(values, ext_width):
    return jnp.repeat(values, ext_width, axis=-1)


def on_device(field, cotangent, mix_weight, taps, offsets, counts):
    lat_dev, lon_dev, channels = field.shape
    lat_count = lax.axis_size("lat")
    lon_count = lax.axis_size("lon")
    total_lat = lat_dev * lat_count
    total_lon = lon_dev * lon_count
    lat_pos = lax.axis_index("lat")
    block_rows = M // lat_count
    chans = channels // lon_count
    first_row = lat_pos * lat_dev
    ext_width = round_up(lon_dev + 2 * R, 16)

    both = jnp.concatenate([field, cotangent], axis=2)
    cosines, log_sines = colatitudes(total_lat)
    orders = lat_pos * block_rows + lax.broadcasted_iota(jnp.int32, (block_rows,), 0)
    own_logs = lax.dynamic_slice_in_dim(seed_logs(M), lat_pos * block_rows, block_rows, 0)
    logscale = own_logs[:, None] + orders.astype(jnp.float32)[:, None] * log_sines[None, :]
    cos_pad, state = legendre_state(cosines, logscale)
    first_order = (lat_pos * block_rows).astype(jnp.int32)
    tables = []

    def next_table(current):
        table, later = legendre_table(first_order, cos_pad, current, len(tables) * DEGREES // LB)
        tables.append(table)
        return later

    before, after = swap_edges(both, "lon", 1, R, True)
    state = next_table(state)
    before, after, state = lax.optimization_barrier((before, after, state))
    spare = jnp.zeros((lat_dev, ext_width - lon_dev - 2 * R, 2 * channels), jnp.bfloat16)
    wide = jnp.concatenate([before, both, after, spare], axis=1)
    above, below = swap_edges(wide, "lat", 0, 1, False)
    state = next_table(state)
    ext = jnp.concatenate([above, wide, below], axis=0).reshape((lat_dev + 2) * ext_width, 2 * channels)

    live = live_taps(taps, counts).astype(jnp.float32)
    live_ext = lax.dynamic_slice_in_dim(jnp.pad(live, ((1, 1), (0, 0), (0, 0), (0, 0))), first_row, lat_dev + 2, 0)
    shift_ext = lax.dynamic_slice_in_dim(jnp.pad(offsets, ((1, 1), (0, 0), (0, 0))), first_row, lat_dev + 2, 0)
    tap_own = spread(jnp.transpose(live_ext[1:-1], (0, 1, 3, 2)), ext_width).reshape(lat_dev, K * S, 3 * ext_width)
    shift_own = spread(jnp.transpose(shift_ext[1:-1], (0, 2, 1)), ext_width)
    live_back = jnp.stack([live_ext[a : a + lat_dev, :, 2 - a, :] for a in range(3)], axis=-1)
    shift_back = jnp.stack([-shift_ext[a : a + lat_dev, 2 - a, :] for a in range(3)], axis=-1)
    tap_back = spread(live_back, ext_width).reshape(lat_dev, K * S, 3 * ext_width)
    shift_back = spread(shift_back, ext_width)

    cot_flat = cotangent.reshape(lat_dev * lon_dev, channels)
    response, grad_field, packed = grid_part(
        ext, cot_flat, mix_weight, tap_own, shift_own, tap_back, shift_back, lon_count
    )

    dft_rows = dft_table(total_lon, orders).reshape(2 * block_rows, total_lon)

    mix_local = lax.dot_general(
        response, cot_flat, (((0,), (0,)), ((), ())), preferred_element_type=jnp.float32
    ) * (1.0 / math.sqrt(total_lat * total_lon))
    mix_rows = K * channels
    split_sum = mix_rows % (lat_count * lon_count) == 0
    if split_sum:
        mix_sent = mix_local.astype(jnp.bfloat16).reshape(lat_count, mix_rows // lat_count, channels)
        packed, mix_sent, mix_local = lax.optimization_barrier((packed, mix_sent, mix_local))
        lat_share = lax.dynamic_index_in_dim(
            mix_local.reshape(lat_count, mix_rows // lat_count, channels), lat_pos, 0, keepdims=False
        )
        arrived = []
        for turn in range(1, lat_count):
            piece = lax.dynamic_index_in_dim(mix_sent, partner(lat_pos, turn, lat_count), 0, keepdims=False)
            arrived.append(swap_with(piece, turn, lat_count))

    columns = lax.all_to_all(packed, "lon", split_axis=0, concat_axis=0, tiled=True)
    columns, state = lax.optimization_barrier((columns, state))
    while len(tables) * DEGREES < L:
        state = next_table(state)
    columns = columns.reshape(total_lon, lat_dev * chans)
    gathered, bands = [columns], [lat_pos]
    for turn in range(1, lat_count):
        gathered.append(swap_with(columns, turn, lat_count))
        bands.append(source_of(lat_pos, turn, lat_count))
    grad_spectra = synthesis(
        jnp.stack(bands).astype(jnp.int32), dft_rows, gathered, tables, chans, total_lat, total_lon
    )

    if split_sum:
        for piece in arrived:
            lat_share = lat_share + piece.astype(jnp.float32)
        lon_rows = mix_rows // (lat_count * lon_count)
        lon_sent = lat_share.astype(jnp.bfloat16).reshape(lon_count, lon_rows, channels)
        lon_got = lax.all_to_all(lon_sent, "lon", split_axis=0, concat_axis=0, tiled=True)
        mix_share = jnp.sum(lon_got.astype(jnp.float32), axis=0).astype(jnp.bfloat16)
        grad_mix = lax.all_gather(mix_share, ("lat", "lon"), axis=0, tiled=False).astype(jnp.float32)
    else:
        grad_mix = lax.psum(mix_local, ("lat", "lon"))
    grad_mix = grad_mix.reshape(K, channels, channels)
    return (grad_field.reshape(lat_dev, lon_dev, channels), grad_spectra, grad_mix)


def solution(mesh):
    placed = (P("lat", "lon", None), P("lat", "lon", None), P(), P(), P(), P())
    return jax.shard_map(
        on_device,
        mesh=mesh,
        in_specs=placed,
        out_specs=(P("lat", "lon", None), P(None, "lat", "lon", None), P()),
        check_vma=False,
    )
```

```python
import functools
import math

import jax
import jax.numpy as jnp
from jax import lax
from jax.experimental import pallas as pl
from jax.experimental.pallas import tpu as pltpu
from jax.sharding import PartitionSpec as P

M = 384
L = 384
K = 3
R = 8
S = 8
LB = 32
MSTEP = 8
DEGREES = 128
PITCH = LB + 1
VMEM_BYTES = 56 * 1024 * 1024


def round_up(value, unit):
    return -(-value // unit) * unit


def live_taps(taps, counts):
    slot_ids = lax.broadcasted_iota(jnp.int32, taps.shape, 3)
    keep_mask = slot_ids < counts[:, None, None, None]
    return jnp.where(keep_mask, taps, jnp.float32(0.0)).astype(jnp.bfloat16)


def dft_table(lon_total, orders):
    columns = lax.broadcasted_iota(jnp.int32, (lon_total,), 0)
    phases = orders[:, None] * columns[None, :] % lon_total
    angles = 2.0 * math.pi / lon_total * phases.astype(jnp.float32)
    return jnp.stack([jnp.cos(angles), -jnp.sin(angles)]).astype(jnp.bfloat16)


def colatitudes(lat_total):
    angles = (lax.broadcasted_iota(jnp.int32, (lat_total,), 0).astype(jnp.float32) + 0.5) * (
        math.pi / lat_total
    )
    return (jnp.cos(angles), jnp.log(jnp.sin(angles)))


def seed_logs(order_total):
    degrees = lax.broadcasted_iota(jnp.int32, (order_total,), 0).astype(jnp.float32)
    step_logs = jnp.log((2.0 * degrees + 1.0) / (2.0 * degrees + 2.0))
    prefix = jnp.concatenate([jnp.zeros((1,), jnp.float32), jnp.cumsum(step_logs)[:-1]])
    return 0.5 * jnp.log((2.0 * degrees + 1.0) / (4.0 * math.pi)) + 0.5 * prefix


def legendre_kernel(start_block, first_ref, cos_ref, prev_in, early_in, scale_in, table_ref, prev_ref, early_ref, scale_ref, *stage_refs):
    step = start_block + pl.program_id(0)
    rows, width = scale_in.shape
    first = first_ref[0]

    @pl.when(pl.program_id(0) == 0)
    def _():
        prev_ref[...] = prev_in[...]
        early_ref[...] = early_in[...]
        scale_ref[...] = scale_in[...]

    chunk = 48 if rows % 48 == 0 else 8
    cosines = cos_ref[...]
    for begin in range(0, rows, chunk):
        span = slice(begin, begin + chunk)
        order_i = lax.broadcasted_iota(jnp.int32, (chunk, LB), 0) + (first + begin)
        degree_i = lax.broadcasted_iota(jnp.int32, (chunk, LB), 1) + step * LB
        order = order_i.astype(jnp.float32)
        degree = degree_i.astype(jnp.float32)
        higher = degree_i > order_i
        lower_a = jnp.where(higher, degree * degree - order * order, 1.0)
        factor_a = jnp.sqrt((4.0 * degree * degree - 1.0) / lower_a)
        upper_b = jnp.maximum((degree - 1.0) * (degree - 1.0) - order * order, 0.0)
        lower_b = jnp.maximum(4.0 * (degree - 1.0) * (degree - 1.0) - 1.0, 1.0)
        factor_b = jnp.sqrt(upper_b / lower_b)
        gain = jnp.where(higher, factor_a, 0.0)
        back = jnp.where(higher, factor_a * factor_b, 0.0)
        wide_order = lax.broadcasted_iota(jnp.int32, (chunk, width), 0) + (first + begin)
        previous = prev_ref[span, :]
        earlier = early_ref[span, :]
        scales = scale_ref[span, :]
        factor = jnp.exp(scales)
        for inner in range(LB):
            seeded = jnp.where(wide_order == step * LB + inner, 1.0, 0.0)
            fresh = (
                gain[:, inner : inner + 1] * (cosines * previous)
                - back[:, inner : inner + 1] * earlier
                + seeded
            )
            level = fresh * factor
            for tile, stage_ref in enumerate(stage_refs):
                stage_ref[pl.ds(begin * PITCH + inner, chunk, stride=PITCH), :] = level[:, tile * 128 : tile * 128 + 128]
            earlier, previous = previous, fresh
        biggest = jnp.maximum(jnp.abs(previous), jnp.abs(earlier))
        divisor = jnp.where(biggest > 0.0, biggest, 1.0)
        prev_ref[span, :] = previous / divisor
        early_ref[span, :] = earlier / divisor
        scale_ref[span, :] = scales + jnp.log(divisor)
    for tile, stage_ref in enumerate(stage_refs):
        for row in range(rows):
            staged = stage_ref[row * PITCH : row * PITCH + LB, :]
            table_ref[row, :, tile * 128 : tile * 128 + 128] = staged.astype(jnp.bfloat16)


def legendre_state(cosines, logscale):
    rows, lat_total = logscale.shape
    spare = round_up(lat_total, 128) - lat_total
    cos_pad = jnp.pad(cosines, (0, spare))[None, :]
    seed_pad = jnp.pad(logscale, ((0, 0), (0, spare)), constant_values=-1.0e4)
    nothing = jnp.zeros_like(seed_pad)
    return cos_pad, (nothing, nothing, seed_pad)


def legendre_table(first_order, cos_pad, state, start_block):
    rows, width = state[0].shape
    plain = pl.BlockSpec((rows, width), lambda i: (0, 0))
    held = jax.ShapeDtypeStruct((rows, width), jnp.float32)
    outs = pl.pallas_call(
        functools.partial(legendre_kernel, start_block),
        grid=(DEGREES // LB,),
        in_specs=[
            pl.BlockSpec(memory_space=pltpu.SMEM),
            pl.BlockSpec((1, width), lambda i: (0, 0)),
            plain,
            plain,
            plain,
        ],
        out_specs=[pl.BlockSpec((rows, LB, width), lambda i: (0, i, 0)), plain, plain, plain],
        out_shape=[jax.ShapeDtypeStruct((rows, DEGREES, width), jnp.bfloat16), held, held, held],
        scratch_shapes=[pltpu.VMEM((rows * PITCH, 128), jnp.float32)] * (width // 128),
        compiler_params=pltpu.CompilerParams(vmem_limit_bytes=VMEM_BYTES),
        cost_estimate=pl.CostEstimate(
            flops=rows * DEGREES * width * 5000, bytes_accessed=rows * DEGREES * width * 2, transcendentals=0
        ),
        name="legendre_table",
    )(first_order.reshape(1), cos_pad, *state)
    return outs[0], tuple(outs[1:])


def synthesis_kernel(lon_total, lat_total, band_count, *refs):
    step = pl.program_id(0)
    band_ref, dft_ref = refs[:2]
    grid_refs = refs[2 : 2 + band_count]
    table_refs = refs[2 + band_count : -2]
    out_ref, modes_ref = refs[-2:]
    packed = grid_refs[0].shape[1]
    rows = dft_ref.shape[0] // 2
    chans = out_ref.shape[2]
    lat_dev = packed // chans
    width = table_refs[0].shape[2]

    @pl.when(step == 0)
    def _():
        for source, grid_ref in enumerate(grid_refs):
            band = band_ref[source]
            modes = jnp.dot(dft_ref[...], grid_ref[...], preferred_element_type=jnp.float32)
            modes = (modes * (1.0 / math.sqrt(lon_total))).astype(jnp.bfloat16).astype(jnp.float32)
            for lat in range(lat_dev):
                dest = pl.ds(pl.multiple_of((band * lat_dev + lat) * rows, 8), rows)
                lanes = slice(lat * chans, (lat + 1) * chans)
                modes_ref[dest, 0:chans] = modes[0:rows, lanes]
                modes_ref[dest, chans : 2 * chans] = modes[rows : 2 * rows, lanes]

    leg_scale = math.sqrt(4.0 * math.pi / lat_total)
    for inner in range(MSTEP):
        picked = modes_ref[pl.ds(step * MSTEP + inner, lat_total, stride=rows), :]
        if width > lat_total:
            spare = jnp.zeros((width - lat_total, picked.shape[1]), jnp.float32)
            picked = jnp.concatenate([picked, spare], axis=0)
        turned = picked.T[0 : 2 * chans].astype(jnp.bfloat16)
        product = lax.dot_general(
            turned,
            jnp.concatenate([table_ref[inner] for table_ref in table_refs], axis=0),
            (((1,), (1,)), ((), ())),
            preferred_element_type=jnp.float32,
        )
        product = product * leg_scale
        out_ref[0, inner] = product[0:chans]
        out_ref[1, inner] = product[chans : 2 * chans]


def synthesis(bands, dft_rows, columns, tables, chans, lat_total, lon_total):
    rows, _, width = tables[0].shape
    whole = lambda i: (0, 0)
    table_spec = pl.BlockSpec((MSTEP, DEGREES, width), lambda i: (i, 0, 0))
    grid_spec = pl.BlockSpec(columns[0].shape, whole, pipeline_mode=pl.Buffered(1))
    return pl.pallas_call(
        functools.partial(synthesis_kernel, lon_total, lat_total, len(columns)),
        grid=(rows // MSTEP,),
        in_specs=[pl.BlockSpec(memory_space=pltpu.SMEM), pl.BlockSpec(dft_rows.shape, whole)]
        + [grid_spec] * len(columns)
        + [table_spec] * len(tables),
        out_specs=pl.BlockSpec((2, MSTEP, chans, L), lambda i: (0, i, 0, 0)),
        out_shape=jax.ShapeDtypeStruct((2, rows, chans, L), jnp.float32),
        scratch_shapes=[pltpu.VMEM((lat_total * rows, 128), jnp.float32)],
        compiler_params=pltpu.CompilerParams(vmem_limit_bytes=VMEM_BYTES),
        cost_estimate=pl.CostEstimate(
            flops=20_000_000_000, bytes_accessed=8 * rows * chans * L, transcendentals=0
        ),
        name="dft_synthesis",
    )(bands, dft_rows, *columns, *tables)


def grid_kernel(
    lon_count, ext_ref, cot_ref, weight_ref, tap_own_ref, shift_own_ref, tap_back_ref, shift_back_ref,
    response_ref, field_ref, send_ref, moved_ref, total_ref, packed_ref,
):
    lat_dev = tap_own_ref.shape[0]
    cells, channels = cot_ref.shape
    lon_dev = cells // lat_dev
    lanes = tap_own_ref.shape[2]
    ext_width = lanes // 3
    lane = lax.broadcasted_iota(jnp.int32, (lon_dev, lanes), 1)
    lane = jnp.where(lane >= 2 * ext_width, lane - 2 * ext_width, jnp.where(lane >= ext_width, lane - ext_width, lane))
    relative = lane - lax.broadcasted_iota(jnp.int32, (lon_dev, lanes), 0) - R

    def bands(row, tap_ref, shift_ref):
        summed = [jnp.zeros((lon_dev, lanes), jnp.float32)] * K
        for slot in range(S):
            hit = relative == shift_ref[row, slot : slot + 1, :]
            for k in range(K):
                tap = tap_ref[row, k * S + slot : k * S + slot + 1, :]
                summed[k] = summed[k] + jnp.where(hit, tap, 0.0)
        return jnp.concatenate(summed, axis=0).astype(jnp.bfloat16)

    @pl.loop(0, lat_dev // 2)
    def _(pair):
        own, back = [], []
        for half in range(2):
            row = pair * 2 + half
            rows = pl.ds(pl.multiple_of(row * ext_width, 16), lanes)
            own.append(
                jnp.dot(
                    bands(row, tap_own_ref, shift_own_ref), ext_ref[rows, 0:channels],
                    preferred_element_type=jnp.float32,
                )
            )
            back.append(
                jnp.dot(
                    bands(row, tap_back_ref, shift_back_ref), ext_ref[rows, channels : 2 * channels],
                    preferred_element_type=jnp.float32,
                )
            )
        dest = pl.ds(pl.multiple_of(pair * 2 * lon_dev, 16), 2 * lon_dev)
        for k in range(K):
            part = slice(k * lon_dev, (k + 1) * lon_dev)
            cols = slice(k * channels, (k + 1) * channels)
            response_ref[dest, cols] = jnp.concatenate([own[0][part], own[1][part]], axis=0).astype(jnp.bfloat16)
            moved_ref[dest, cols] = jnp.concatenate([back[0][part], back[1][part]], axis=0).astype(jnp.bfloat16)

    total = cot_ref[...].astype(jnp.float32)
    for k in range(K):
        total = total + lax.dot_general(
            moved_ref[:, k * channels : (k + 1) * channels], weight_ref[k],
            (((1,), (1,)), ((), ())), preferred_element_type=jnp.float32,
        )
    rounded = total.astype(jnp.bfloat16)
    field_ref[...] = rounded
    total_ref[...] = rounded.astype(jnp.float32)
    chans = channels // lon_count
    for lat in range(lat_dev):
        for dest in range(lon_count):
            packed_ref[dest, :, lat * chans : (lat + 1) * chans] = total_ref[
                lat * lon_dev : (lat + 1) * lon_dev, dest * chans : (dest + 1) * chans
            ]
    send_ref[...] = packed_ref[...].astype(jnp.bfloat16)


def grid_part(ext, cot, mix_weight, tap_own, shift_own, tap_back, shift_back, lon_count):
    cells, channels = cot.shape
    lat_dev = tap_own.shape[0]
    lon_dev = cells // lat_dev
    packed = (lon_count, lon_dev, lat_dev * (channels // lon_count))
    return pl.pallas_call(
        functools.partial(grid_kernel, lon_count),
        in_specs=[pl.BlockSpec(memory_space=pltpu.VMEM)] * 7,
        out_specs=[pl.BlockSpec(memory_space=pltpu.VMEM)] * 3,
        out_shape=[
            jax.ShapeDtypeStruct((cells, K * channels), jnp.bfloat16),
            jax.ShapeDtypeStruct((cells, channels), jnp.bfloat16),
            jax.ShapeDtypeStruct(packed, jnp.bfloat16),
        ],
        scratch_shapes=[
            pltpu.VMEM((cells, K * channels), jnp.bfloat16),
            pltpu.VMEM((cells, channels), jnp.float32),
            pltpu.VMEM(packed, jnp.float32),
        ],
        compiler_params=pltpu.CompilerParams(vmem_limit_bytes=VMEM_BYTES),
        name="grid_part",
    )(ext, cot, mix_weight, tap_own, shift_own, tap_back, shift_back)


def swap_edges(shard, axis, dim, width, wrap):
    devices, length = lax.axis_size(axis), shard.shape[dim]
    up = [(i, (i + 1) % devices) for i in range(devices if wrap else devices - 1)]
    down = [(j, i) for i, j in up]
    before = lax.ppermute(lax.slice_in_dim(shard, length - width, length, axis=dim), axis, up)
    after = lax.ppermute(lax.slice_in_dim(shard, 0, width, axis=dim), axis, down)
    return before, after


def partner(position, turn, count):
    if count & (count - 1) == 0:
        return position ^ turn
    return (position + turn) % count


def source_of(position, turn, count):
    if count & (count - 1) == 0:
        return position ^ turn
    return (position + count - turn) % count


def swap_with(value, turn, count):
    return lax.ppermute(value, "lat", [(i, partner(i, turn, count)) for i in range(count)])


def spread(values, ext_width):
    return jnp.repeat(values, ext_width, axis=-1)


def on_device(field, cotangent, mix_weight, taps, offsets, counts):
    lat_dev, lon_dev, channels = field.shape
    lat_count = lax.axis_size("lat")
    lon_count = lax.axis_size("lon")
    total_lat = lat_dev * lat_count
    total_lon = lon_dev * lon_count
    lat_pos = lax.axis_index("lat")
    block_rows = M // lat_count
    chans = channels // lon_count
    first_row = lat_pos * lat_dev
    ext_width = round_up(lon_dev + 2 * R, 16)

    both = jnp.concatenate([field, cotangent], axis=2)
    cosines, log_sines = colatitudes(total_lat)
    orders = lat_pos * block_rows + lax.broadcasted_iota(jnp.int32, (block_rows,), 0)
    own_logs = lax.dynamic_slice_in_dim(seed_logs(M), lat_pos * block_rows, block_rows, 0)
    logscale = own_logs[:, None] + orders.astype(jnp.float32)[:, None] * log_sines[None, :]
    cos_pad, state = legendre_state(cosines, logscale)
    first_order = (lat_pos * block_rows).astype(jnp.int32)
    tables = []

    def next_table(current):
        table, later = legendre_table(first_order, cos_pad, current, len(tables) * DEGREES // LB)
        tables.append(table)
        return later

    live = live_taps(taps, counts).astype(jnp.float32)
    live_ext = lax.dynamic_slice_in_dim(jnp.pad(live, ((1, 1), (0, 0), (0, 0), (0, 0))), first_row, lat_dev + 2, 0)
    shift_ext = lax.dynamic_slice_in_dim(jnp.pad(offsets, ((1, 1), (0, 0), (0, 0))), first_row, lat_dev + 2, 0)
    tap_own = spread(jnp.transpose(live_ext[1:-1], (0, 1, 3, 2)), ext_width).reshape(lat_dev, K * S, 3 * ext_width)
    shift_own = spread(jnp.transpose(shift_ext[1:-1], (0, 2, 1)), ext_width)
    live_back = jnp.stack([live_ext[a : a + lat_dev, :, 2 - a, :] for a in range(3)], axis=-1)
    shift_back = jnp.stack([-shift_ext[a : a + lat_dev, 2 - a, :] for a in range(3)], axis=-1)
    tap_back = spread(live_back, ext_width).reshape(lat_dev, K * S, 3 * ext_width)
    shift_back = spread(shift_back, ext_width)

    before, after = swap_edges(both, "lon", 1, R, True)
    rows_of_taps = (tap_own, shift_own, tap_back, shift_back)
    before, after, rows_of_taps = lax.optimization_barrier((before, after, rows_of_taps))
    spare = jnp.zeros((lat_dev, ext_width - lon_dev - 2 * R, 2 * channels), jnp.bfloat16)
    wide = jnp.concatenate([before, both, after, spare], axis=1)
    above, below = swap_edges(wide, "lat", 0, 1, False)
    ext = jnp.concatenate([above, wide, below], axis=0).reshape((lat_dev + 2) * ext_width, 2 * channels)

    cot_flat = cotangent.reshape(lat_dev * lon_dev, channels)
    response, grad_field, packed = grid_part(
        ext, cot_flat, mix_weight, *rows_of_taps, lon_count
    )
    packed, state = lax.optimization_barrier((packed, state))
    state = next_table(state)

    dft_rows = dft_table(total_lon, orders).reshape(2 * block_rows, total_lon)

    mix_local = lax.dot_general(
        response, cot_flat, (((0,), (0,)), ((), ())), preferred_element_type=jnp.float32
    ) * (1.0 / math.sqrt(total_lat * total_lon))
    mix_rows = K * channels
    split_sum = mix_rows % (lat_count * lon_count) == 0
    if split_sum:
        mix_sent = mix_local.astype(jnp.bfloat16).reshape(lat_count, mix_rows // lat_count, channels)
        lat_share = lax.dynamic_index_in_dim(
            mix_local.reshape(lat_count, mix_rows // lat_count, channels), lat_pos, 0, keepdims=False
        )
        arrived = []
        for turn in range(1, lat_count):
            piece = lax.dynamic_index_in_dim(mix_sent, partner(lat_pos, turn, lat_count), 0, keepdims=False)
            arrived.append(swap_with(piece, turn, lat_count))

    columns = lax.all_to_all(packed, "lon", split_axis=0, concat_axis=0, tiled=True)
    columns, state = lax.optimization_barrier((columns, state))
    state = next_table(state)
    columns = columns.reshape(total_lon, lat_dev * chans)
    gathered, bands = [columns], [lat_pos]
    for turn in range(1, lat_count):
        gathered.append(swap_with(columns, turn, lat_count))
        bands.append(source_of(lat_pos, turn, lat_count))
    if split_sum:
        for piece in arrived:
            lat_share = lat_share + piece.astype(jnp.float32)
        lon_rows = mix_rows // (lat_count * lon_count)
        lon_sent = lat_share.astype(jnp.bfloat16).reshape(lon_count, lon_rows, channels)
        lon_got = lax.all_to_all(lon_sent, "lon", split_axis=0, concat_axis=0, tiled=True)
        lon_got, state = lax.optimization_barrier((lon_got, state))
        mix_share = jnp.sum(lon_got.astype(jnp.float32), axis=0).astype(jnp.bfloat16)
        copies = jnp.broadcast_to(mix_share[None], lon_got.shape)
        mix_band = lax.all_to_all(copies, "lon", split_axis=0, concat_axis=0, tiled=True)
    while len(tables) * DEGREES < L:
        state = next_table(state)
    if split_sum:
        gathered, tables, mix_band = lax.optimization_barrier((gathered, tables, mix_band))
        mix_bands = [mix_band] + [swap_with(mix_band, turn, lat_count) for turn in range(1, lat_count)]
    grad_spectra = synthesis(
        jnp.stack(bands).astype(jnp.int32), dft_rows, gathered, tables, chans, total_lat, total_lon
    )

    if split_sum:
        ordered = []
        for band in range(lat_count):
            chosen = mix_bands[0]
            for turn in range(1, lat_count):
                chosen = jnp.where(source_of(lat_pos, turn, lat_count) == band, mix_bands[turn], chosen)
            ordered.append(chosen.astype(jnp.float32))
        grad_mix = jnp.stack(ordered)
    else:
        grad_mix = lax.psum(mix_local, ("lat", "lon"))
    grad_mix = grad_mix.reshape(K, channels, channels)
    return (grad_field.reshape(lat_dev, lon_dev, channels), grad_spectra, grad_mix)


def solution(mesh):
    placed = (P("lat", "lon", None), P("lat", "lon", None), P(), P(), P(), P())
    return jax.shard_map(
        on_device,
        mesh=mesh,
        in_specs=placed,
        out_specs=(P("lat", "lon", None), P(None, "lat", "lon", None), P()),
        check_vma=False,
    )
```

```python
import functools
import math

import jax
import jax.numpy as jnp
from jax import lax
from jax.experimental import pallas as pl
from jax.experimental.pallas import tpu as pltpu
from jax.sharding import PartitionSpec as P

M = 384
L = 384
K = 3
R = 8
S = 8
LB = 32
MSTEP = 8
DEGREES = 128
PITCH = LB + 1
VMEM_BYTES = 56 * 1024 * 1024


def round_up(value, unit):
    return -(-value // unit) * unit


def live_taps(taps, counts):
    slot_ids = lax.broadcasted_iota(jnp.int32, taps.shape, 3)
    keep_mask = slot_ids < counts[:, None, None, None]
    return jnp.where(keep_mask, taps, jnp.float32(0.0)).astype(jnp.bfloat16)


def dft_table(lon_total, orders):
    columns = lax.broadcasted_iota(jnp.int32, (lon_total,), 0)
    phases = orders[:, None] * columns[None, :] % lon_total
    angles = 2.0 * math.pi / lon_total * phases.astype(jnp.float32)
    return jnp.stack([jnp.cos(angles), -jnp.sin(angles)]).astype(jnp.bfloat16)


def colatitudes(lat_total):
    angles = (lax.broadcasted_iota(jnp.int32, (lat_total,), 0).astype(jnp.float32) + 0.5) * (
        math.pi / lat_total
    )
    return (jnp.cos(angles), jnp.log(jnp.sin(angles)))


def seed_logs(order_total):
    degrees = lax.broadcasted_iota(jnp.int32, (order_total,), 0).astype(jnp.float32)
    step_logs = jnp.log((2.0 * degrees + 1.0) / (2.0 * degrees + 2.0))
    prefix = jnp.concatenate([jnp.zeros((1,), jnp.float32), jnp.cumsum(step_logs)[:-1]])
    return 0.5 * jnp.log((2.0 * degrees + 1.0) / (4.0 * math.pi)) + 0.5 * prefix


def legendre_kernel(start_block, first_ref, cos_ref, prev_in, early_in, scale_in, table_ref, prev_ref, early_ref, scale_ref, *stage_refs):
    step = start_block + pl.program_id(0)
    rows, width = scale_in.shape
    first = first_ref[0]

    @pl.when(pl.program_id(0) == 0)
    def _():
        prev_ref[...] = prev_in[...]
        early_ref[...] = early_in[...]
        scale_ref[...] = scale_in[...]

    chunk = 48 if rows % 48 == 0 else 8
    cosines = cos_ref[...]
    for begin in range(0, rows, chunk):
        span = slice(begin, begin + chunk)
        order_i = lax.broadcasted_iota(jnp.int32, (chunk, LB), 0) + (first + begin)
        degree_i = lax.broadcasted_iota(jnp.int32, (chunk, LB), 1) + step * LB
        order = order_i.astype(jnp.float32)
        degree = degree_i.astype(jnp.float32)
        higher = degree_i > order_i
        lower_a = jnp.where(higher, degree * degree - order * order, 1.0)
        factor_a = jnp.sqrt((4.0 * degree * degree - 1.0) / lower_a)
        upper_b = jnp.maximum((degree - 1.0) * (degree - 1.0) - order * order, 0.0)
        lower_b = jnp.maximum(4.0 * (degree - 1.0) * (degree - 1.0) - 1.0, 1.0)
        factor_b = jnp.sqrt(upper_b / lower_b)
        gain = jnp.where(higher, factor_a, 0.0)
        back = jnp.where(higher, factor_a * factor_b, 0.0)
        wide_order = lax.broadcasted_iota(jnp.int32, (chunk, width), 0) + (first + begin)
        previous = prev_ref[span, :]
        earlier = early_ref[span, :]
        scales = scale_ref[span, :]
        factor = jnp.exp(scales)
        for inner in range(LB):
            seeded = jnp.where(wide_order == step * LB + inner, 1.0, 0.0)
            fresh = (
                gain[:, inner : inner + 1] * (cosines * previous)
                - back[:, inner : inner + 1] * earlier
                + seeded
            )
            level = fresh * factor
            for tile, stage_ref in enumerate(stage_refs):
                stage_ref[pl.ds(begin * PITCH + inner, chunk, stride=PITCH), :] = level[:, tile * 128 : tile * 128 + 128]
            earlier, previous = previous, fresh
        biggest = jnp.maximum(jnp.abs(previous), jnp.abs(earlier))
        divisor = jnp.where(biggest > 0.0, biggest, 1.0)
        prev_ref[span, :] = previous / divisor
        early_ref[span, :] = earlier / divisor
        scale_ref[span, :] = scales + jnp.log(divisor)
    for tile, stage_ref in enumerate(stage_refs):
        for row in range(rows):
            staged = stage_ref[row * PITCH : row * PITCH + LB, :]
            table_ref[row, :, tile * 128 : tile * 128 + 128] = staged.astype(jnp.bfloat16)


def legendre_state(cosines, logscale):
    rows, lat_total = logscale.shape
    spare = round_up(lat_total, 128) - lat_total
    cos_pad = jnp.pad(cosines, (0, spare))[None, :]
    seed_pad = jnp.pad(logscale, ((0, 0), (0, spare)), constant_values=-1.0e4)
    nothing = jnp.zeros_like(seed_pad)
    return cos_pad, (nothing, nothing, seed_pad)


def legendre_table(first_order, cos_pad, state, start_block):
    rows, width = state[0].shape
    plain = pl.BlockSpec((rows, width), lambda i: (0, 0))
    held = jax.ShapeDtypeStruct((rows, width), jnp.float32)
    outs = pl.pallas_call(
        functools.partial(legendre_kernel, start_block),
        grid=(DEGREES // LB,),
        in_specs=[
            pl.BlockSpec(memory_space=pltpu.SMEM),
            pl.BlockSpec((1, width), lambda i: (0, 0)),
            plain,
            plain,
            plain,
        ],
        out_specs=[pl.BlockSpec((rows, LB, width), lambda i: (0, i, 0)), plain, plain, plain],
        out_shape=[jax.ShapeDtypeStruct((rows, DEGREES, width), jnp.bfloat16), held, held, held],
        scratch_shapes=[pltpu.VMEM((rows * PITCH, 128), jnp.float32)] * (width // 128),
        compiler_params=pltpu.CompilerParams(vmem_limit_bytes=VMEM_BYTES),
        cost_estimate=pl.CostEstimate(
            flops=rows * DEGREES * width * 5000, bytes_accessed=rows * DEGREES * width * 2, transcendentals=0
        ),
        name="legendre_table",
    )(first_order.reshape(1), cos_pad, *state)
    return outs[0], tuple(outs[1:])


def synthesis_kernel(lon_total, lat_total, band_count, *refs):
    step = pl.program_id(0)
    band_ref, dft_ref = refs[:2]
    grid_refs = refs[2 : 2 + band_count]
    table_refs = refs[2 + band_count : -2]
    out_ref, modes_ref = refs[-2:]
    packed = grid_refs[0].shape[1]
    rows = dft_ref.shape[0] // 2
    chans = out_ref.shape[2]
    lat_dev = packed // chans
    width = table_refs[0].shape[2]

    @pl.when(step == 0)
    def _():
        for source, grid_ref in enumerate(grid_refs):
            band = band_ref[source]
            modes = jnp.dot(dft_ref[...], grid_ref[...], preferred_element_type=jnp.float32)
            modes = (modes * (1.0 / math.sqrt(lon_total))).astype(jnp.bfloat16).astype(jnp.float32)
            for lat in range(lat_dev):
                dest = pl.ds(pl.multiple_of((band * lat_dev + lat) * rows, 8), rows)
                lanes = slice(lat * chans, (lat + 1) * chans)
                modes_ref[dest, 0:chans] = modes[0:rows, lanes]
                modes_ref[dest, chans : 2 * chans] = modes[rows : 2 * rows, lanes]

    leg_scale = math.sqrt(4.0 * math.pi / lat_total)
    for inner in range(MSTEP):
        picked = modes_ref[pl.ds(step * MSTEP + inner, lat_total, stride=rows), :]
        if width > lat_total:
            spare = jnp.zeros((width - lat_total, picked.shape[1]), jnp.float32)
            picked = jnp.concatenate([picked, spare], axis=0)
        turned = picked.T[0 : 2 * chans].astype(jnp.bfloat16)
        product = lax.dot_general(
            turned,
            jnp.concatenate([table_ref[inner] for table_ref in table_refs], axis=0),
            (((1,), (1,)), ((), ())),
            preferred_element_type=jnp.float32,
        )
        product = product * leg_scale
        out_ref[0, inner] = product[0:chans]
        out_ref[1, inner] = product[chans : 2 * chans]


def synthesis(bands, dft_rows, columns, tables, chans, lat_total, lon_total):
    rows, _, width = tables[0].shape
    whole = lambda i: (0, 0)
    table_spec = pl.BlockSpec((MSTEP, DEGREES, width), lambda i: (i, 0, 0))
    grid_spec = pl.BlockSpec(columns[0].shape, whole, pipeline_mode=pl.Buffered(1))
    return pl.pallas_call(
        functools.partial(synthesis_kernel, lon_total, lat_total, len(columns)),
        grid=(rows // MSTEP,),
        in_specs=[pl.BlockSpec(memory_space=pltpu.SMEM), pl.BlockSpec(dft_rows.shape, whole)]
        + [grid_spec] * len(columns)
        + [table_spec] * len(tables),
        out_specs=pl.BlockSpec((2, MSTEP, chans, L), lambda i: (0, i, 0, 0)),
        out_shape=jax.ShapeDtypeStruct((2, rows, chans, L), jnp.float32),
        scratch_shapes=[pltpu.VMEM((lat_total * rows, 128), jnp.float32)],
        compiler_params=pltpu.CompilerParams(vmem_limit_bytes=VMEM_BYTES),
        cost_estimate=pl.CostEstimate(
            flops=20_000_000_000, bytes_accessed=8 * rows * chans * L, transcendentals=0
        ),
        name="dft_synthesis",
    )(bands, dft_rows, *columns, *tables)


def grid_kernel(
    lon_count, ext_ref, cot_ref, weight_ref, tap_ref, shift_ref,
    response_ref, field_ref, send_ref, moved_ref, total_ref, packed_ref,
):
    lat_dev = tap_ref.shape[0] - 2
    cells, channels = cot_ref.shape
    lon_dev = cells // lat_dev
    ext_width = ext_ref.shape[0] // (lat_dev + 2)
    lanes = 3 * ext_width
    place = lax.broadcasted_iota(jnp.int32, (1, lanes), 1)
    at_first, at_second = place < ext_width, place < 2 * ext_width
    lane = lax.broadcasted_iota(jnp.int32, (lon_dev, lanes), 1)
    lane = jnp.where(lane >= 2 * ext_width, lane - 2 * ext_width, jnp.where(lane >= ext_width, lane - ext_width, lane))
    relative = lane - lax.broadcasted_iota(jnp.int32, (lon_dev, lanes), 0) - R

    def across(three):
        return jnp.where(at_first, three[0], jnp.where(at_second, three[1], three[2]))

    def bands(row, adjoint):
        if adjoint:
            sources = [(row + a, 2 - a) for a in range(3)]
        else:
            sources = [(row + 1, a) for a in range(3)]
        summed = [jnp.zeros((lon_dev, lanes), jnp.float32)] * K
        for slot in range(S):
            shift = across([shift_ref[source, a * S + slot] for source, a in sources])
            hit = relative == (-shift if adjoint else shift)
            for k in range(K):
                tap = across([tap_ref[source, (k * 3 + a) * S + slot] for source, a in sources])
                summed[k] = summed[k] + jnp.where(hit, tap, 0.0)
        return jnp.concatenate(summed, axis=0).astype(jnp.bfloat16)

    @pl.loop(0, lat_dev // 2)
    def _(pair):
        own, back = [], []
        for half in range(2):
            row = pair * 2 + half
            rows = pl.ds(pl.multiple_of(row * ext_width, 16), lanes)
            own.append(
                jnp.dot(
                    bands(row, False), ext_ref[rows, 0:channels],
                    preferred_element_type=jnp.float32,
                )
            )
            back.append(
                jnp.dot(
                    bands(row, True), ext_ref[rows, channels : 2 * channels],
                    preferred_element_type=jnp.float32,
                )
            )
        dest = pl.ds(pl.multiple_of(pair * 2 * lon_dev, 16), 2 * lon_dev)
        for k in range(K):
            part = slice(k * lon_dev, (k + 1) * lon_dev)
            cols = slice(k * channels, (k + 1) * channels)
            response_ref[dest, cols] = jnp.concatenate([own[0][part], own[1][part]], axis=0).astype(jnp.bfloat16)
            moved_ref[dest, cols] = jnp.concatenate([back[0][part], back[1][part]], axis=0).astype(jnp.bfloat16)

    total = cot_ref[...].astype(jnp.float32)
    for k in range(K):
        total = total + lax.dot_general(
            moved_ref[:, k * channels : (k + 1) * channels], weight_ref[k],
            (((1,), (1,)), ((), ())), preferred_element_type=jnp.float32,
        )
    rounded = total.astype(jnp.bfloat16)
    field_ref[...] = rounded
    total_ref[...] = rounded.astype(jnp.float32)
    chans = channels // lon_count
    for lat in range(lat_dev):
        for dest in range(lon_count):
            packed_ref[dest, :, lat * chans : (lat + 1) * chans] = total_ref[
                lat * lon_dev : (lat + 1) * lon_dev, dest * chans : (dest + 1) * chans
            ]
    send_ref[...] = packed_ref[...].astype(jnp.bfloat16)


def grid_part(ext, cot, mix_weight, taps, shifts, lon_count):
    cells, channels = cot.shape
    lat_dev = taps.shape[0] - 2
    lon_dev = cells // lat_dev
    packed = (lon_count, lon_dev, lat_dev * (channels // lon_count))
    return pl.pallas_call(
        functools.partial(grid_kernel, lon_count),
        in_specs=[pl.BlockSpec(memory_space=pltpu.VMEM)] * 3 + [pl.BlockSpec(memory_space=pltpu.SMEM)] * 2,
        out_specs=[pl.BlockSpec(memory_space=pltpu.VMEM)] * 3,
        out_shape=[
            jax.ShapeDtypeStruct((cells, K * channels), jnp.bfloat16),
            jax.ShapeDtypeStruct((cells, channels), jnp.bfloat16),
            jax.ShapeDtypeStruct(packed, jnp.bfloat16),
        ],
        scratch_shapes=[
            pltpu.VMEM((cells, K * channels), jnp.bfloat16),
            pltpu.VMEM((cells, channels), jnp.float32),
            pltpu.VMEM(packed, jnp.float32),
        ],
        compiler_params=pltpu.CompilerParams(vmem_limit_bytes=VMEM_BYTES),
        name="grid_part",
    )(ext, cot, mix_weight, taps, shifts)


def swap_edges(shard, axis, dim, width, wrap):
    devices, length = lax.axis_size(axis), shard.shape[dim]
    up = [(i, (i + 1) % devices) for i in range(devices if wrap else devices - 1)]
    down = [(j, i) for i, j in up]
    before = lax.ppermute(lax.slice_in_dim(shard, length - width, length, axis=dim), axis, up)
    after = lax.ppermute(lax.slice_in_dim(shard, 0, width, axis=dim), axis, down)
    return before, after


def partner(position, turn, count):
    if count & (count - 1) == 0:
        return position ^ turn
    return (position + turn) % count


def source_of(position, turn, count):
    if count & (count - 1) == 0:
        return position ^ turn
    return (position + count - turn) % count


def swap_with(value, turn, count):
    return lax.ppermute(value, "lat", [(i, partner(i, turn, count)) for i in range(count)])


def on_device(field, cotangent, mix_weight, taps, offsets, counts):
    lat_dev, lon_dev, channels = field.shape
    lat_count = lax.axis_size("lat")
    lon_count = lax.axis_size("lon")
    total_lat = lat_dev * lat_count
    total_lon = lon_dev * lon_count
    lat_pos = lax.axis_index("lat")
    block_rows = M // lat_count
    chans = channels // lon_count
    first_row = lat_pos * lat_dev
    ext_width = round_up(lon_dev + 2 * R, 16)

    both = jnp.concatenate([field, cotangent], axis=2)
    cosines, log_sines = colatitudes(total_lat)
    orders = lat_pos * block_rows + lax.broadcasted_iota(jnp.int32, (block_rows,), 0)
    own_logs = lax.dynamic_slice_in_dim(seed_logs(M), lat_pos * block_rows, block_rows, 0)
    logscale = own_logs[:, None] + orders.astype(jnp.float32)[:, None] * log_sines[None, :]
    cos_pad, state = legendre_state(cosines, logscale)
    first_order = (lat_pos * block_rows).astype(jnp.int32)
    tables = []

    def next_table(current):
        table, later = legendre_table(first_order, cos_pad, current, len(tables) * DEGREES // LB)
        tables.append(table)
        return later

    live = live_taps(taps, counts).astype(jnp.float32).reshape(total_lat, K * 3 * S)
    live_ext = lax.dynamic_slice_in_dim(jnp.pad(live, ((1, 1), (0, 0))), first_row, lat_dev + 2, 0)
    shift_pad = jnp.pad(offsets.reshape(total_lat, 3 * S), ((1, 1), (0, 0)))
    shift_ext = lax.dynamic_slice_in_dim(shift_pad, first_row, lat_dev + 2, 0)

    before, after = swap_edges(both, "lon", 1, R, True)
    state = next_table(state)
    before, after, live_ext, shift_ext, state = lax.optimization_barrier(
        (before, after, live_ext, shift_ext, state)
    )
    spare = jnp.zeros((lat_dev, ext_width - lon_dev - 2 * R, 2 * channels), jnp.bfloat16)
    wide = jnp.concatenate([before, both, after, spare], axis=1)
    above, below = swap_edges(wide, "lat", 0, 1, False)
    ext = jnp.concatenate([above, wide, below], axis=0).reshape((lat_dev + 2) * ext_width, 2 * channels)

    cot_flat = cotangent.reshape(lat_dev * lon_dev, channels)
    response, grad_field, packed = grid_part(
        ext, cot_flat, mix_weight, live_ext, shift_ext, lon_count
    )
    packed, state = lax.optimization_barrier((packed, state))
    state = next_table(state)

    dft_rows = dft_table(total_lon, orders).reshape(2 * block_rows, total_lon)

    mix_local = lax.dot_general(
        response, cot_flat, (((0,), (0,)), ((), ())), preferred_element_type=jnp.float32
    ) * (1.0 / math.sqrt(total_lat * total_lon))
    mix_rows = K * channels
    split_sum = mix_rows % (lat_count * lon_count) == 0
    if split_sum:
        mix_sent = mix_local.astype(jnp.bfloat16).reshape(lat_count, mix_rows // lat_count, channels)
        lat_share = lax.dynamic_index_in_dim(
            mix_local.reshape(lat_count, mix_rows // lat_count, channels), lat_pos, 0, keepdims=False
        )
        arrived = []
        for turn in range(1, lat_count):
            piece = lax.dynamic_index_in_dim(mix_sent, partner(lat_pos, turn, lat_count), 0, keepdims=False)
            arrived.append(swap_with(piece, turn, lat_count))

    columns = lax.all_to_all(packed, "lon", split_axis=0, concat_axis=0, tiled=True)
    columns, state = lax.optimization_barrier((columns, state))
    state = next_table(state)
    columns = columns.reshape(total_lon, lat_dev * chans)
    gathered, bands = [columns], [lat_pos]
    for turn in range(1, lat_count):
        gathered.append(swap_with(columns, turn, lat_count))
        bands.append(source_of(lat_pos, turn, lat_count))
    if split_sum:
        for piece in arrived:
            lat_share = lat_share + piece.astype(jnp.float32)
        lon_rows = mix_rows // (lat_count * lon_count)
        lon_sent = lat_share.astype(jnp.bfloat16).reshape(lon_count, lon_rows, channels)
        lon_got = lax.all_to_all(lon_sent, "lon", split_axis=0, concat_axis=0, tiled=True)
        lon_got, state = lax.optimization_barrier((lon_got, state))
        mix_share = jnp.sum(lon_got.astype(jnp.float32), axis=0).astype(jnp.bfloat16)
        copies = jnp.broadcast_to(mix_share[None], lon_got.shape)
        mix_band = lax.all_to_all(copies, "lon", split_axis=0, concat_axis=0, tiled=True)
    while len(tables) * DEGREES < L:
        state = next_table(state)
    if split_sum:
        gathered, tables, mix_band = lax.optimization_barrier((gathered, tables, mix_band))
        mix_bands = [mix_band] + [swap_with(mix_band, turn, lat_count) for turn in range(1, lat_count)]
    grad_spectra = synthesis(
        jnp.stack(bands).astype(jnp.int32), dft_rows, gathered, tables, chans, total_lat, total_lon
    )

    if split_sum:
        ordered = []
        for band in range(lat_count):
            chosen = mix_bands[0]
            for turn in range(1, lat_count):
                chosen = jnp.where(source_of(lat_pos, turn, lat_count) == band, mix_bands[turn], chosen)
            ordered.append(chosen.astype(jnp.float32))
        grad_mix = jnp.stack(ordered)
    else:
        grad_mix = lax.psum(mix_local, ("lat", "lon"))
    grad_mix = grad_mix.reshape(K, channels, channels)
    return (grad_field.reshape(lat_dev, lon_dev, channels), grad_spectra, grad_mix)


def solution(mesh):
    placed = (P("lat", "lon", None), P("lat", "lon", None), P(), P(), P(), P())
    return jax.shard_map(
        on_device,
        mesh=mesh,
        in_specs=placed,
        out_specs=(P("lat", "lon", None), P(None, "lat", "lon", None), P()),
        check_vma=False,
    )
```

```python
import functools
import math

import jax
import jax.numpy as jnp
from jax import lax
from jax.experimental import pallas as pl
from jax.experimental.pallas import tpu as pltpu
from jax.sharding import PartitionSpec as P

M = 384
L = 384
K = 3
R = 8
S = 8
LB = 32
MSTEP = 8
DEGREES = 128
PITCH = LB + 1
VMEM_BYTES = 56 * 1024 * 1024


def round_up(value, unit):
    return -(-value // unit) * unit


def live_taps(taps, counts):
    slot_ids = lax.broadcasted_iota(jnp.int32, taps.shape, 3)
    keep_mask = slot_ids < counts[:, None, None, None]
    return jnp.where(keep_mask, taps, jnp.float32(0.0)).astype(jnp.bfloat16)


def dft_table(lon_total, orders):
    columns = lax.broadcasted_iota(jnp.int32, (lon_total,), 0)
    phases = orders[:, None] * columns[None, :] % lon_total
    angles = 2.0 * math.pi / lon_total * phases.astype(jnp.float32)
    return jnp.stack([jnp.cos(angles), -jnp.sin(angles)]).astype(jnp.bfloat16)


def colatitudes(lat_total):
    angles = (lax.broadcasted_iota(jnp.int32, (lat_total,), 0).astype(jnp.float32) + 0.5) * (
        math.pi / lat_total
    )
    return (jnp.cos(angles), jnp.log(jnp.sin(angles)))


def seed_logs(order_total):
    degrees = lax.broadcasted_iota(jnp.int32, (order_total,), 0).astype(jnp.float32)
    step_logs = jnp.log((2.0 * degrees + 1.0) / (2.0 * degrees + 2.0))
    prefix = jnp.concatenate([jnp.zeros((1,), jnp.float32), jnp.cumsum(step_logs)[:-1]])
    return 0.5 * jnp.log((2.0 * degrees + 1.0) / (4.0 * math.pi)) + 0.5 * prefix


def legendre_kernel(start_block, first_ref, cos_ref, prev_in, early_in, scale_in, table_ref, prev_ref, early_ref, scale_ref, *stage_refs):
    step = start_block + pl.program_id(0)
    rows, width = scale_in.shape
    first = first_ref[0]

    @pl.when(pl.program_id(0) == 0)
    def _():
        prev_ref[...] = prev_in[...]
        early_ref[...] = early_in[...]
        scale_ref[...] = scale_in[...]

    chunk = 48 if rows % 48 == 0 else 8
    cosines = cos_ref[...]
    for begin in range(0, rows, chunk):
        span = slice(begin, begin + chunk)
        order_i = lax.broadcasted_iota(jnp.int32, (chunk, LB), 0) + (first + begin)
        degree_i = lax.broadcasted_iota(jnp.int32, (chunk, LB), 1) + step * LB
        order = order_i.astype(jnp.float32)
        degree = degree_i.astype(jnp.float32)
        higher = degree_i > order_i
        lower_a = jnp.where(higher, degree * degree - order * order, 1.0)
        factor_a = jnp.sqrt((4.0 * degree * degree - 1.0) / lower_a)
        upper_b = jnp.maximum((degree - 1.0) * (degree - 1.0) - order * order, 0.0)
        lower_b = jnp.maximum(4.0 * (degree - 1.0) * (degree - 1.0) - 1.0, 1.0)
        factor_b = jnp.sqrt(upper_b / lower_b)
        gain = jnp.where(higher, factor_a, 0.0)
        back = jnp.where(higher, factor_a * factor_b, 0.0)
        wide_order = lax.broadcasted_iota(jnp.int32, (chunk, width), 0) + (first + begin)
        previous = prev_ref[span, :]
        earlier = early_ref[span, :]
        scales = scale_ref[span, :]
        factor = jnp.exp(scales)
        for inner in range(LB):
            seeded = jnp.where(wide_order == step * LB + inner, 1.0, 0.0)
            fresh = (
                gain[:, inner : inner + 1] * (cosines * previous)
                - back[:, inner : inner + 1] * earlier
                + seeded
            )
            level = fresh * factor
            for tile, stage_ref in enumerate(stage_refs):
                stage_ref[pl.ds(begin * PITCH + inner, chunk, stride=PITCH), :] = level[:, tile * 128 : tile * 128 + 128]
            earlier, previous = previous, fresh
        biggest = jnp.maximum(jnp.abs(previous), jnp.abs(earlier))
        divisor = jnp.where(biggest > 0.0, biggest, 1.0)
        prev_ref[span, :] = previous / divisor
        early_ref[span, :] = earlier / divisor
        scale_ref[span, :] = scales + jnp.log(divisor)
    for tile, stage_ref in enumerate(stage_refs):
        for row in range(rows):
            staged = stage_ref[row * PITCH : row * PITCH + LB, :]
            table_ref[row, :, tile * 128 : tile * 128 + 128] = staged.astype(jnp.bfloat16)


def legendre_state(cosines, logscale):
    rows, lat_total = logscale.shape
    spare = round_up(lat_total, 128) - lat_total
    cos_pad = jnp.pad(cosines, (0, spare))[None, :]
    seed_pad = jnp.pad(logscale, ((0, 0), (0, spare)), constant_values=-1.0e4)
    nothing = jnp.zeros_like(seed_pad)
    return cos_pad, (nothing, nothing, seed_pad)


def legendre_table(first_order, cos_pad, state, start_block):
    rows, width = state[0].shape
    plain = pl.BlockSpec((rows, width), lambda i: (0, 0))
    held = jax.ShapeDtypeStruct((rows, width), jnp.float32)
    outs = pl.pallas_call(
        functools.partial(legendre_kernel, start_block),
        grid=(DEGREES // LB,),
        in_specs=[
            pl.BlockSpec(memory_space=pltpu.SMEM),
            pl.BlockSpec((1, width), lambda i: (0, 0)),
            plain,
            plain,
            plain,
        ],
        out_specs=[pl.BlockSpec((rows, LB, width), lambda i: (0, i, 0)), plain, plain, plain],
        out_shape=[jax.ShapeDtypeStruct((rows, DEGREES, width), jnp.bfloat16), held, held, held],
        scratch_shapes=[pltpu.VMEM((rows * PITCH, 128), jnp.float32)] * (width // 128),
        compiler_params=pltpu.CompilerParams(vmem_limit_bytes=VMEM_BYTES),
        cost_estimate=pl.CostEstimate(
            flops=rows * DEGREES * width * 5000, bytes_accessed=rows * DEGREES * width * 2, transcendentals=0
        ),
        name="legendre_table",
    )(first_order.reshape(1), cos_pad, *state)
    return outs[0], tuple(outs[1:])


def synthesis_kernel(lon_total, lat_total, band_count, *refs):
    step = pl.program_id(0)
    band_ref, dft_ref = refs[:2]
    grid_refs = refs[2 : 2 + band_count]
    table_refs = refs[2 + band_count : -2]
    out_ref, modes_ref = refs[-2:]
    packed = grid_refs[0].shape[1]
    rows = dft_ref.shape[0] // 2
    chans = out_ref.shape[2]
    lat_dev = packed // chans
    width = table_refs[0].shape[2]

    @pl.when(step == 0)
    def _():
        for source, grid_ref in enumerate(grid_refs):
            band = band_ref[source]
            modes = jnp.dot(dft_ref[...], grid_ref[...], preferred_element_type=jnp.float32)
            modes = (modes * (1.0 / math.sqrt(lon_total))).astype(jnp.bfloat16).astype(jnp.float32)
            for lat in range(lat_dev):
                dest = pl.ds(pl.multiple_of((band * lat_dev + lat) * rows, 8), rows)
                lanes = slice(lat * chans, (lat + 1) * chans)
                modes_ref[dest, 0:chans] = modes[0:rows, lanes]
                modes_ref[dest, chans : 2 * chans] = modes[rows : 2 * rows, lanes]

    leg_scale = math.sqrt(4.0 * math.pi / lat_total)
    for inner in range(MSTEP):
        picked = modes_ref[pl.ds(step * MSTEP + inner, lat_total, stride=rows), :]
        if width > lat_total:
            spare = jnp.zeros((width - lat_total, picked.shape[1]), jnp.float32)
            picked = jnp.concatenate([picked, spare], axis=0)
        turned = picked.T[0 : 2 * chans].astype(jnp.bfloat16)
        product = lax.dot_general(
            turned,
            jnp.concatenate([table_ref[inner] for table_ref in table_refs], axis=0),
            (((1,), (1,)), ((), ())),
            preferred_element_type=jnp.float32,
        )
        product = product * leg_scale
        out_ref[0, inner] = product[0:chans]
        out_ref[1, inner] = product[chans : 2 * chans]


def synthesis(bands, dft_rows, columns, tables, chans, lat_total, lon_total):
    rows, _, width = tables[0].shape
    whole = lambda i: (0, 0)
    table_spec = pl.BlockSpec((MSTEP, DEGREES, width), lambda i: (i, 0, 0))
    grid_spec = pl.BlockSpec(columns[0].shape, whole, pipeline_mode=pl.Buffered(1))
    return pl.pallas_call(
        functools.partial(synthesis_kernel, lon_total, lat_total, len(columns)),
        grid=(rows // MSTEP,),
        in_specs=[pl.BlockSpec(memory_space=pltpu.SMEM), pl.BlockSpec(dft_rows.shape, whole)]
        + [grid_spec] * len(columns)
        + [table_spec] * len(tables),
        out_specs=pl.BlockSpec((2, MSTEP, chans, L), lambda i: (0, i, 0, 0)),
        out_shape=jax.ShapeDtypeStruct((2, rows, chans, L), jnp.float32),
        scratch_shapes=[pltpu.VMEM((lat_total * rows, 128), jnp.float32)],
        compiler_params=pltpu.CompilerParams(vmem_limit_bytes=VMEM_BYTES),
        cost_estimate=pl.CostEstimate(
            flops=20_000_000_000, bytes_accessed=8 * rows * chans * L, transcendentals=0
        ),
        name="dft_synthesis",
    )(bands, dft_rows, *columns, *tables)


def grid_kernel(
    lon_count, ext_ref, cot_ref, weight_ref, tap_ref, shift_ref,
    response_ref, field_ref, send_ref, moved_ref, total_ref, packed_ref,
):
    lat_dev = tap_ref.shape[0] - 2
    cells, channels = cot_ref.shape
    lon_dev = cells // lat_dev
    ext_width = ext_ref.shape[0] // (lat_dev + 2)
    lanes = 3 * ext_width
    place = lax.broadcasted_iota(jnp.int32, (1, lanes), 1)
    at_first, at_second = place < ext_width, place < 2 * ext_width
    lane = lax.broadcasted_iota(jnp.int32, (lon_dev, lanes), 1)
    lane = jnp.where(lane >= 2 * ext_width, lane - 2 * ext_width, jnp.where(lane >= ext_width, lane - ext_width, lane))
    relative = lane - lax.broadcasted_iota(jnp.int32, (lon_dev, lanes), 0) - R

    def across(three):
        return jnp.where(at_first, three[0], jnp.where(at_second, three[1], three[2]))

    def bands(row, adjoint):
        if adjoint:
            sources = [(row + a, 2 - a) for a in range(3)]
        else:
            sources = [(row + 1, a) for a in range(3)]
        summed = [jnp.zeros((lon_dev, lanes), jnp.float32)] * K
        for slot in range(S):
            shift = across([shift_ref[source, a * S + slot] for source, a in sources])
            hit = relative == (-shift if adjoint else shift)
            for k in range(K):
                tap = across([tap_ref[source, (k * 3 + a) * S + slot] for source, a in sources])
                summed[k] = summed[k] + jnp.where(hit, tap, 0.0)
        return jnp.concatenate(summed, axis=0).astype(jnp.bfloat16)

    @pl.loop(0, lat_dev // 2)
    def _(pair):
        own, back = [], []
        for half in range(2):
            row = pair * 2 + half
            rows = pl.ds(pl.multiple_of(row * ext_width, 16), lanes)
            own.append(
                jnp.dot(
                    bands(row, False), ext_ref[rows, 0:channels],
                    preferred_element_type=jnp.float32,
                )
            )
            back.append(
                jnp.dot(
                    bands(row, True), ext_ref[rows, channels : 2 * channels],
                    preferred_element_type=jnp.float32,
                )
            )
        dest = pl.ds(pl.multiple_of(pair * 2 * lon_dev, 16), 2 * lon_dev)
        for k in range(K):
            part = slice(k * lon_dev, (k + 1) * lon_dev)
            cols = slice(k * channels, (k + 1) * channels)
            response_ref[dest, cols] = jnp.concatenate([own[0][part], own[1][part]], axis=0).astype(jnp.bfloat16)
            moved_ref[dest, cols] = jnp.concatenate([back[0][part], back[1][part]], axis=0).astype(jnp.bfloat16)

    total = cot_ref[...].astype(jnp.float32)
    for k in range(K):
        total = total + lax.dot_general(
            moved_ref[:, k * channels : (k + 1) * channels], weight_ref[k],
            (((1,), (1,)), ((), ())), preferred_element_type=jnp.float32,
        )
    rounded = total.astype(jnp.bfloat16)
    field_ref[...] = rounded
    total_ref[...] = rounded.astype(jnp.float32)
    chans = channels // lon_count
    for lat in range(lat_dev):
        for dest in range(lon_count):
            packed_ref[dest, :, lat * chans : (lat + 1) * chans] = total_ref[
                lat * lon_dev : (lat + 1) * lon_dev, dest * chans : (dest + 1) * chans
            ]
    send_ref[...] = packed_ref[...].astype(jnp.bfloat16)


def grid_part(ext, cot, mix_weight, taps, shifts, lon_count):
    cells, channels = cot.shape
    lat_dev = taps.shape[0] - 2
    lon_dev = cells // lat_dev
    packed = (lon_count, lon_dev, lat_dev * (channels // lon_count))
    return pl.pallas_call(
        functools.partial(grid_kernel, lon_count),
        in_specs=[pl.BlockSpec(memory_space=pltpu.VMEM)] * 3 + [pl.BlockSpec(memory_space=pltpu.SMEM)] * 2,
        out_specs=[pl.BlockSpec(memory_space=pltpu.VMEM)] * 3,
        out_shape=[
            jax.ShapeDtypeStruct((cells, K * channels), jnp.bfloat16),
            jax.ShapeDtypeStruct((cells, channels), jnp.bfloat16),
            jax.ShapeDtypeStruct(packed, jnp.bfloat16),
        ],
        scratch_shapes=[
            pltpu.VMEM((cells, K * channels), jnp.bfloat16),
            pltpu.VMEM((cells, channels), jnp.float32),
            pltpu.VMEM(packed, jnp.float32),
        ],
        compiler_params=pltpu.CompilerParams(vmem_limit_bytes=VMEM_BYTES),
        name="grid_part",
    )(ext, cot, mix_weight, taps, shifts)


def swap_edges(shard, axis, dim, width, wrap):
    devices, length = lax.axis_size(axis), shard.shape[dim]
    up = [(i, (i + 1) % devices) for i in range(devices if wrap else devices - 1)]
    down = [(j, i) for i, j in up]
    before = lax.ppermute(lax.slice_in_dim(shard, length - width, length, axis=dim), axis, up)
    after = lax.ppermute(lax.slice_in_dim(shard, 0, width, axis=dim), axis, down)
    return before, after


def partner(position, turn, count):
    if count & (count - 1) == 0:
        return position ^ turn
    return (position + turn) % count


def source_of(position, turn, count):
    if count & (count - 1) == 0:
        return position ^ turn
    return (position + count - turn) % count


def swap_with(value, turn, count):
    return lax.ppermute(value, "lat", [(i, partner(i, turn, count)) for i in range(count)])


def on_device(field, cotangent, mix_weight, taps, offsets, counts):
    lat_dev, lon_dev, channels = field.shape
    lat_count = lax.axis_size("lat")
    lon_count = lax.axis_size("lon")
    total_lat = lat_dev * lat_count
    total_lon = lon_dev * lon_count
    lat_pos = lax.axis_index("lat")
    block_rows = M // lat_count
    chans = channels // lon_count
    first_row = lat_pos * lat_dev
    ext_width = round_up(lon_dev + 2 * R, 16)

    both = jnp.concatenate([field, cotangent], axis=2)
    cosines, log_sines = colatitudes(total_lat)
    orders = lat_pos * block_rows + lax.broadcasted_iota(jnp.int32, (block_rows,), 0)
    own_logs = lax.dynamic_slice_in_dim(seed_logs(M), lat_pos * block_rows, block_rows, 0)
    logscale = own_logs[:, None] + orders.astype(jnp.float32)[:, None] * log_sines[None, :]
    cos_pad, state = legendre_state(cosines, logscale)
    first_order = (lat_pos * block_rows).astype(jnp.int32)
    tables = []

    def next_table(current):
        table, later = legendre_table(first_order, cos_pad, current, len(tables) * DEGREES // LB)
        tables.append(table)
        return later

    live = live_taps(taps, counts).astype(jnp.float32).reshape(total_lat, K * 3 * S)
    live_ext = lax.dynamic_slice_in_dim(jnp.pad(live, ((1, 1), (0, 0))), first_row, lat_dev + 2, 0)
    shift_pad = jnp.pad(offsets.reshape(total_lat, 3 * S), ((1, 1), (0, 0)))
    shift_ext = lax.dynamic_slice_in_dim(shift_pad, first_row, lat_dev + 2, 0)

    before, after = swap_edges(both, "lon", 1, R, True)
    state = next_table(state)
    before, after, live_ext, shift_ext, state = lax.optimization_barrier(
        (before, after, live_ext, shift_ext, state)
    )
    spare = jnp.zeros((lat_dev, ext_width - lon_dev - 2 * R, 2 * channels), jnp.bfloat16)
    wide = jnp.concatenate([before, both, after, spare], axis=1)
    above, below = swap_edges(wide, "lat", 0, 1, False)
    ext = jnp.concatenate([above, wide, below], axis=0).reshape((lat_dev + 2) * ext_width, 2 * channels)

    cot_flat = cotangent.reshape(lat_dev * lon_dev, channels)
    response, grad_field, packed = grid_part(
        ext, cot_flat, mix_weight, live_ext, shift_ext, lon_count
    )
    packed, state = lax.optimization_barrier((packed, state))
    state = next_table(state)

    dft_rows = dft_table(total_lon, orders).reshape(2 * block_rows, total_lon)

    mix_local = lax.dot_general(
        response, cot_flat, (((0,), (0,)), ((), ())), preferred_element_type=jnp.float32
    ) * (1.0 / math.sqrt(total_lat * total_lon))
    mix_rows = K * channels
    arrived = []
    split_sum = mix_rows % (lat_count * lon_count) == 0
    if split_sum:
        mix_sent = mix_local.astype(jnp.bfloat16).reshape(lat_count, mix_rows // lat_count, channels)
        lat_share = lax.dynamic_index_in_dim(
            mix_local.reshape(lat_count, mix_rows // lat_count, channels), lat_pos, 0, keepdims=False
        )
        for turn in range(1, lat_count):
            piece = lax.dynamic_index_in_dim(mix_sent, partner(lat_pos, turn, lat_count), 0, keepdims=False)
            arrived.append(swap_with(piece, turn, lat_count))

    columns = lax.all_to_all(packed, "lon", split_axis=0, concat_axis=0, tiled=True)
    columns, state, arrived = lax.optimization_barrier((columns, state, arrived))
    state = next_table(state)
    columns = columns.reshape(total_lon, lat_dev * chans)
    gathered, bands = [columns], [lat_pos]
    for turn in range(1, lat_count):
        gathered.append(swap_with(columns, turn, lat_count))
        bands.append(source_of(lat_pos, turn, lat_count))
    if split_sum:
        for piece in arrived:
            lat_share = lat_share + piece.astype(jnp.float32)
        lon_rows = mix_rows // (lat_count * lon_count)
        lon_sent = lat_share.astype(jnp.bfloat16).reshape(lon_count, lon_rows, channels)
        lon_got = lax.all_to_all(lon_sent, "lon", split_axis=0, concat_axis=0, tiled=True)
        lon_got, state = lax.optimization_barrier((lon_got, state))
        mix_share = jnp.sum(lon_got.astype(jnp.float32), axis=0).astype(jnp.bfloat16)
        copies = jnp.broadcast_to(mix_share[None], lon_got.shape)
        mix_band = lax.all_to_all(copies, "lon", split_axis=0, concat_axis=0, tiled=True)
    while len(tables) * DEGREES < L:
        state = next_table(state)
    if split_sum:
        gathered, tables, mix_band = lax.optimization_barrier((gathered, tables, mix_band))
        mix_bands = [mix_band] + [swap_with(mix_band, turn, lat_count) for turn in range(1, lat_count)]
    grad_spectra = synthesis(
        jnp.stack(bands).astype(jnp.int32), dft_rows, gathered, tables, chans, total_lat, total_lon
    )

    if split_sum:
        ordered = []
        for band in range(lat_count):
            chosen = mix_bands[0]
            for turn in range(1, lat_count):
                chosen = jnp.where(source_of(lat_pos, turn, lat_count) == band, mix_bands[turn], chosen)
            ordered.append(chosen.astype(jnp.float32))
        grad_mix = jnp.stack(ordered)
    else:
        grad_mix = lax.psum(mix_local, ("lat", "lon"))
    grad_mix = grad_mix.reshape(K, channels, channels)
    return (grad_field.reshape(lat_dev, lon_dev, channels), grad_spectra, grad_mix)


def solution(mesh):
    placed = (P("lat", "lon", None), P("lat", "lon", None), P(), P(), P(), P())
    return jax.shard_map(
        on_device,
        mesh=mesh,
        in_specs=placed,
        out_specs=(P("lat", "lon", None), P(None, "lat", "lon", None), P()),
        check_vma=False,
    )
```
